256 devices in a mesh: rep: 16 (over x, z_lo, core), fsdp: 16 (over y, z_hi).
Axes of the slice: x: 4, y: 4, z: 8 (z_hi: 4, z_lo: 2; z = z_hi * 2 + z_lo), core: 2. Of those that a mesh axis runs over, the one named last changes fastest.
Arguments:
- tokens: bfloat16 [131072, 2560], P(('rep', 'fsdp')), may hold values from -6 to 6
- out_grads: bfloat16 [131072, 4096], P(('rep', 'fsdp')), may hold values from -0.625 to 0.625
- weight: bfloat16 [4096, 2560], P('fsdp'), may hold values from -0.75 to 0.75
- momentum: bfloat16 [16, 4096, 2560], P('rep', 'fsdp'), may hold values from -6 to 6
- kept_blocks: int32 [16, 64, 40, 4], P('rep', 'fsdp'), may hold values from 0 to 63, as said below
Outputs:
- new_weight: bfloat16 [4096, 2560], P('fsdp')
- new_momentum: bfloat16 [16, 4096, 2560], P('rep', 'fsdp')
The draws below stay inside these ranges and needn't reach their ends.
Inputs may be any that keep to these rules, and one draw needn't show every extreme that they name: `kept_blocks`: the 4 block numbers of each span of each replica are distinct.
All inputs are finite; a program needn't handle non-finite values.
Results may differ from the reference program's by a relative error of at most 0.015.
Values may be sent and summed in bfloat16 or wider, within the bound.
A program may use at most 128 MiB of HBM per device.

```python
import jax
import jax.numpy as jnp
from jax import lax

D = 2560
F = 4096
TOK_DEV = 512
KEEP = 4
REPS = 16
TOKENS = 131072
N_FSDP = 16


def draw_kept_blocks(key, part):
    key = jax.random.fold_in(key, 11)
    scores = jax.random.randint(key, (REPS, F // 64, D // 64, 64), 0, 1 << 20, dtype=jnp.int32)
    scores = scores * 64 + jnp.arange(64, dtype=jnp.int32)
    ordering = jnp.argsort(scores, axis=-1)
    return ordering[..., :KEEP].astype(jnp.int32)


def spiked(values, rng, source, target, blocks, factor):
    owner, partner = [(jnp.arange(values.shape[axis_at]) // (values.shape[axis_at] // blocks)).reshape([-1 if axis == axis_at else 1 for axis in range(values.ndim)]) for axis_at in (source, target)]
    chosen = jax.random.permutation(rng, blocks)[partner]
    strong = (owner == chosen) | (owner == (partner + blocks // 2) % blocks)
    return jnp.where(strong, factor * values, values)


def block_levels(own_key, extent, shards, least, top_value):
    loudness = 1.0
    for axis_at, parts in shards:
        heights = jax.random.uniform(jax.random.fold_in(jax.random.fold_in(own_key, 6), axis_at), (parts,), jnp.float32, least / len(shards), top_value / len(shards))
        loudness = loudness * jnp.repeat(jnp.exp(heights), extent[axis_at] // parts).reshape((-1,) + (1,) * (len(extent) - 1 - axis_at))
    return loudness


def centred(own_key, extent, spread, limit, pieces=(), kind=jnp.bfloat16):
    array = jax.random.normal(own_key, extent, jnp.float32) * spread
    if len(pieces) > 0:
        array = block_levels(own_key, extent, pieces, -0.22, 0.18) * array
    return jnp.clip(array, min=-limit, max=limit).astype(kind)


def noise_with(key, extent, scale, bound, split, heavy, kind=jnp.bfloat16):
    result = scale * jax.random.normal(key, extent, jnp.float32)
    if split:
        result = result * block_levels(key, extent, split, -0.22, 0.18)
    return jnp.clip(spiked(result, jax.random.fold_in(key, 3), *heavy), -bound, bound).astype(kind)


def setup_inputs(seed: int = 0) -> dict:
    splits = jax.random.split(jax.random.key(seed), 6)
    return {
        "tokens": centred(splits[0], (TOKENS, D), 1.0, 6.0, ((0, 256),)),
        "out_grads": noise_with(splits[1], (TOKENS, F), ((TOK_DEV * N_FSDP) ** -0.5), 0.625, ((0, 256),), (0, 1, 256, 6.0)),
        "weight": centred(splits[2], (F, D), 0.05, 0.75, ((0, 16),)),
        "momentum": centred(splits[3], (REPS, F, D), 1.0, 6.0, ((0, 16), (1, 16))),
        "kept_blocks": draw_kept_blocks(jax.random.fold_in(splits[5], 71), 0),
    }


beta_decay = 0.9
step_rate = 0.5

def dct_table():
    position = jnp.arange(64, dtype=jnp.float32)
    frequency = position[:, None]
    scaling = jnp.where(frequency == 0, jnp.sqrt(1.0 / 64.0), jnp.sqrt(2.0 / 64.0))
    return (scaling * jnp.cos(jnp.pi * (2.0 * position[None, :] + 1.0) * frequency / 128.0)).astype(jnp.float32)

def to_cells(field, row_blocks, col_blocks):
    shaped = field.reshape(row_blocks, 64, col_blocks, 64)
    return shaped.transpose(1, 3, 0, 2).reshape(64, 64, row_blocks * col_blocks)

def from_cells(cells, row_blocks, col_blocks):
    shaped = cells.reshape(64, 64, row_blocks, col_blocks)
    return shaped.transpose(2, 0, 3, 1).reshape(row_blocks * 64, col_blocks * 64)

def forward(cells, cosine_table):
    halfway = jnp.einsum('ki,ijc->kjc', cosine_table, cells, precision=lax.Precision.HIGHEST)
    spectra = jnp.einsum('lj,kjc->klc', cosine_table, halfway, precision=lax.Precision.HIGHEST)
    spans = spectra.shape[2]
    return spectra.reshape(8, 8, 8, 8, spans).transpose(0, 2, 1, 3, 4).reshape(64, 64, spans)

def inverse(blocked, cosine_table):
    spans = blocked.shape[2]
    spectra = blocked.reshape(8, 8, 8, 8, spans).transpose(0, 2, 1, 3, 4).reshape(64, 64, spans)
    halfway = jnp.einsum('ki,klc->ilc', cosine_table, spectra, precision=lax.Precision.HIGHEST)
    return jnp.einsum('lj,ilc->ijc', cosine_table, halfway, precision=lax.Precision.HIGHEST)

def block_mask(chosen):
    numbers = jnp.arange(64, dtype=jnp.int32)
    return (chosen[None, :, :] == numbers[:, None, None]).astype(jnp.float32)

def pick_blocks(blocked, chosen):
    return jnp.einsum('bkc,bwc->kwc', block_mask(chosen), blocked, precision=lax.Precision.HIGHEST)

def place_blocks(picked, chosen):
    return jnp.einsum('bkc,kwc->bwc', block_mask(chosen), picked, precision=lax.Precision.HIGHEST)

def reference(tokens, out_grads, weight, momentum, kept_blocks):
    cosine_table = dct_table()
    row_blocks = F // 64
    col_blocks = D // 64
    grouped_tokens = tokens.reshape(REPS, N_FSDP, TOK_DEV, D)
    grouped_grads = out_grads.reshape(REPS, N_FSDP, TOK_DEV, F)

    def one_replica(running, element):
        rep_tokens, rep_grads, prior, selection = element

        def add_partial(gradient, slices):
            partial_value = lax.dot_general(slices[1].astype(jnp.float32), slices[0].astype(jnp.float32), (((0,), (0,)), ((), ())))
            rounded = lax.optimization_barrier(partial_value.astype(jnp.bfloat16))
            return (gradient + rounded.astype(jnp.float32), None)
        gradient, unused = lax.scan(add_partial, jnp.zeros((F, D), jnp.float32), (rep_tokens, rep_grads))
        moment = beta_decay * prior.astype(jnp.float32) + gradient
        blocked = forward(to_cells(moment, row_blocks, col_blocks), cosine_table)
        chosen = selection.reshape(row_blocks * col_blocks, KEEP).T.astype(jnp.int32)
        own_sparse = place_blocks(pick_blocks(blocked, chosen), chosen)
        removed = from_cells(inverse(own_sparse, cosine_table), row_blocks, col_blocks)
        fresh = (moment - removed).astype(jnp.bfloat16)
        return (running + own_sparse, fresh)
    start_sum = jnp.zeros((64, 64, row_blocks * col_blocks), jnp.float32)
    summed_coeffs, new_momentum = lax.scan(one_replica, start_sum, (grouped_tokens, grouped_grads, momentum, kept_blocks))
    update = from_cells(inverse(summed_coeffs, cosine_table), row_blocks, col_blocks) / REPS
    new_weight = (weight.astype(jnp.float32) - step_rate * update).astype(jnp.bfloat16)
    return (new_weight, new_momentum)
```

```python
import functools

import jax
import jax.numpy as jnp
import numpy as np
from jax import lax
from jax.experimental import pallas as pl
from jax.experimental.pallas import tpu as pltpu
from jax.sharding import PartitionSpec as P

beta_decay = 0.9
step_rate = 0.5

MESH = pl.DeviceIdType.MESH
F32 = jnp.float32
BF16 = jnp.bfloat16

D = 2560
ROWS = 256
SIDE = 4
REPS = 16

JOBS = (
    ("y", 0, 1024, 256),
    ("y", 256, 1280, 256),
    ("y", 512, 1536, 256),
    ("y", 768, 1792, 128),
    ("y", 896, 1920, 128),
    ("z", 2048, 2304, 256),
)
ORDER = (
    (0, 0), (0, 5), (1, 0), (0, 1), (1, 5), (2, 0), (1, 1), (0, 2), (2, 1), (2, 5),
    (1, 2), (0, 3), (3, 0), (2, 2), (1, 3), (0, 4), (3, 5), (3, 1), (4, 0), (2, 3),
    (1, 4), (4, 5), (4, 1), (3, 2), (2, 4), (3, 3), (4, 2), (3, 4), (4, 3), (4, 4),
)


def scatter_kernel(g_hbm, t_ref, out_ref, gt, stage, load_sem, send_sem, recv_sem, *bufs):
    wide, thin = bufs[: len(JOBS)], bufs[len(JOBS) :]
    rep = lax.axis_index("rep")
    member = lax.axis_index("fsdp")
    pos = {"y": member // SIDE, "z": member % SIDE}

    def device(axis, index):
        if axis == "y":
            return (rep, index * SIDE + pos["z"])
        return (rep, pos["y"] * SIDE + index)

    def turn(index, by):
        return lax.rem(index + (by + SIDE), SIDE)

    loads = []
    for block in range(SIDE):
        group = turn(pos["y"], 2 + block)
        loads.append(
            pltpu.make_async_copy(
                g_hbm.at[:, pl.ds(pl.multiple_of(group * 1024, 1024), 1024)],
                stage.at[block],
                load_sem.at[block],
            )
        )
        loads[-1].start()

    barrier = pltpu.get_barrier_semaphore()
    for axis in ("y", "z"):
        for by in (1, -1):
            pl.semaphore_signal(
                barrier, inc=1, device_id=device(axis, turn(pos[axis], by)), device_id_type=MESH
            )
    pl.semaphore_wait(barrier, 4)

    for block in range(SIDE):
        group = turn(pos["y"], 2 + block)
        loads[block].wait()

        @pl.loop(0, SIDE)
        def _(part, block=block, group=group):
            start = pl.multiple_of(group * 1024 + part * ROWS, ROWS)
            gt[pl.ds(start, ROWS), :] = stage[
                block, :, pl.ds(pl.multiple_of(part * ROWS, ROWS), ROWS)
            ].T

    def partial(axis, group, other, column, width):
        owner = group * SIDE + other if axis == "y" else other * SIDE + group
        rows = pl.ds(pl.multiple_of(owner * ROWS, ROWS), ROWS)
        return jnp.dot(
            gt[rows, :], t_ref[:, column : column + width], preferred_element_type=F32
        )

    sent = []

    def send(src, dst, job, side, number, target):
        copy = pltpu.make_async_remote_copy(
            src_ref=src,
            dst_ref=dst,
            send_sem=send_sem.at[job, side, number],
            recv_sem=recv_sem.at[job, side, number],
            device_id=target,
            device_id_type=MESH,
        )
        copy.start()
        sent.append(copy)

    def arrived(dst, job, side, number):
        pltpu.make_async_remote_copy(
            src_ref=dst,
            dst_ref=dst,
            send_sem=send_sem.at[job, side, number],
            recv_sem=recv_sem.at[job, side, number],
            device_id=(rep, member),
            device_id_type=MESH,
        ).wait_recv()

    for step, job in ORDER:
        axis, column_a, column_b, width = JOBS[job]
        other_axis = "z" if axis == "y" else "y"
        m, n = pos[axis], pos[other_axis]
        sides = ((0, column_a, -1), (1, column_b, 1))
        if step == 0:
            for slot in (0, 1):
                for side, column, d in sides:
                    buf = wide[job].at[side]
                    group, target = (turn(m, 2), turn(m, d)) if slot == 0 else (turn(m, -d),) * 2

                    @pl.loop(0, SIDE)
                    def _(other, buf=buf, group=group, column=column, slot=slot):
                        buf[slot, other] = partial(axis, group, other, column, width).astype(BF16)

                    send(buf.at[slot], buf.at[slot + 2], job, side, slot, device(axis, target))
        elif step == 1:
            for side, column, d in sides:
                buf = wide[job].at[side]
                arrived(buf.at[2], job, side, 0)

                @pl.loop(0, SIDE)
                def _(other, buf=buf, group=turn(m, d), column=column):
                    total = partial(axis, group, other, column, width) + buf[2, other].astype(F32)
                    buf[2, other] = total.astype(BF16)

                send(buf.at[2], buf.at[4], job, side, 2, device(axis, turn(m, d)))
        elif step == 2:
            for side, column, d in sides:
                buf, low = wide[job].at[side], thin[job].at[side]
                arrived(buf.at[3], job, side, 1)
                arrived(buf.at[4], job, side, 2)
                for slot, other in ((0, turn(n, 2)), (1, turn(n, -d)), (2, turn(n, d)), (3, n)):
                    total = (
                        partial(axis, m, other, column, width)
                        + buf[3, other].astype(F32)
                        + buf[4, other].astype(F32)
                    )
                    if slot == 3:
                        out_ref[:, column : column + width] = total
                    else:
                        low[slot] = total.astype(BF16)
                    if slot < 2:
                        target = turn(n, d) if slot == 0 else turn(n, -d)
                        send(
                            low.at[slot],
                            low.at[slot + 3],
                            job,
                            side,
                            slot + 3,
                            device(other_axis, target),
                        )
        elif step == 3:
            for side, column, d in sides:
                low = thin[job].at[side]
                arrived(low.at[3], job, side, 3)
                low[3] = (low[2].astype(F32) + low[3].astype(F32)).astype(BF16)
                send(low.at[3], low.at[5], job, side, 5, device(other_axis, turn(n, d)))
        else:
            for side, column, d in sides:
                low = thin[job].at[side]
                arrived(low.at[4], job, side, 4)
                arrived(low.at[5], job, side, 5)
                out_ref[:, column : column + width] += low[4].astype(F32) + low[5].astype(F32)

    for copy in sent:
        copy.wait_send()


def reduced_gradient(out_grads, tokens):
    vmem = pl.BlockSpec(memory_space=pltpu.VMEM)
    return pl.pallas_call(
        scatter_kernel,
        out_shape=jax.ShapeDtypeStruct((ROWS, D), F32),
        in_specs=[pl.BlockSpec(memory_space=pl.ANY), vmem],
        out_specs=vmem,
        scratch_shapes=[
            pltpu.VMEM((4096, 512), BF16),
            pltpu.VMEM((SIDE, 512, 1024), BF16),
            pltpu.SemaphoreType.DMA((SIDE,)),
            pltpu.SemaphoreType.DMA((len(JOBS), 2, 6)),
            pltpu.SemaphoreType.DMA((len(JOBS), 2, 6)),
        ]
        + [pltpu.VMEM((2, 5, SIDE, ROWS, job[3]), BF16) for job in JOBS]
        + [pltpu.VMEM((2, 6, ROWS, job[3]), BF16) for job in JOBS],
        compiler_params=pltpu.CompilerParams(
            collective_id=0, has_side_effects=True, vmem_limit_bytes=60 * 2**20
        ),
        cost_estimate=pl.CostEstimate(
            flops=2 * 512 * 4096 * D, bytes_accessed=2 * 512 * (4096 + D), transcendentals=0
        ),
    )(out_grads, tokens)


def split_dot(left, right):
    total = jnp.dot(left[0], right[0], preferred_element_type=F32)
    total += jnp.dot(left[0], right[1], preferred_element_type=F32)
    return total + jnp.dot(left[1], right[0], preferred_element_type=F32)


def halves(value):
    high = value.astype(BF16)
    return high, (value - high.astype(F32)).astype(BF16)


def codec_kernel(
    grad_ref, mom_ref, own_ref, kept_ref, weight_ref, table_ref, fold_ref, spread_ref,
    new_weight_ref, new_mom_ref,
    picked, packed, packed_in, kept_in, tile,
    kept_send, kept_recv, pack_send, pack_recv, tile_send, tile_recv,
):
    rep = lax.axis_index("rep")
    member = lax.axis_index("fsdp")

    def peer(by):
        return lax.rem(rep + by, REPS)

    barrier = pltpu.get_barrier_semaphore()
    for by in range(1, REPS):
        pl.semaphore_signal(barrier, inc=1, device_id=(peer(by), member), device_id_type=MESH)
    pl.semaphore_wait(barrier, REPS - 1)

    def copy_to(src, dst, send_sem, recv_sem, target):
        return pltpu.make_async_remote_copy(
            src_ref=src, dst_ref=dst, send_sem=send_sem, recv_sem=recv_sem,
            device_id=(target, member), device_id_type=MESH,
        )

    sent = []
    for by in range(1, REPS):
        copy = copy_to(
            kept_ref.at[peer(by)], kept_in.at[by], kept_send.at[by], kept_recv.at[by], peer(by)
        )
        copy.start()
        sent.append(copy)

    forward = table_ref[0], table_ref[1]
    backward = table_ref[2], table_ref[3]
    column_block = lax.rem(lax.broadcasted_iota(jnp.int32, (1, 640), 1), 64) // 8

    @pl.loop(0, D // 256)
    def _(index):
        columns = pl.ds(pl.multiple_of(index * 256, 256), 256)
        moment = beta_decay * mom_ref[:, columns].astype(F32) + grad_ref[:, columns]
        halfway = split_dot(forward, halves(moment))
        coeffs = split_dot(halves(halfway), backward)
        sparse_rows = []
        for a in range(4):
            numbers = [own_ref[a, k : k + 1, columns] for k in range(4)]
            folded = [jnp.zeros((8, 256), F32)] * 4
            for r in range(8):
                piece = coeffs[64 * a + 8 * r : 64 * a + 8 * r + 8, :]
                here = column_block[:, :256] + 8 * r
                kept = jnp.zeros((8, 256), F32)
                for k in range(4):
                    one = jnp.where(numbers[k] == here, piece, 0.0)
                    folded[k] += one
                    kept += one
                sparse_rows.append(kept)
            picked[a, :, columns] = jnp.concatenate(folded, axis=0).astype(BF16)
        sparse = jnp.concatenate(sparse_rows, axis=0)
        halfway = split_dot(backward, halves(sparse))
        removed = split_dot(halves(halfway), forward)
        new_mom_ref[:, columns] = (moment - removed).astype(BF16)

    for c in range(4):
        for a in range(4):
            packed[a * 4 + c] = jnp.dot(
                picked[a, :, 640 * c : 640 * c + 640], fold_ref[...], preferred_element_type=F32
            ).astype(BF16)
    for by in range(1, REPS):
        copy = copy_to(
            packed.at[peer(by)], packed_in.at[by], pack_send.at[by], pack_recv.at[by], peer(by)
        )
        copy.start()
        sent.append(copy)
    packed_in[0] = packed[rep]
    kept_in[0] = kept_ref[rep]
    for by in range(1, REPS):
        copy_to(
            kept_in.at[by], kept_in.at[by], kept_send.at[by], kept_recv.at[by], peer(by)
        ).wait_recv()
        copy_to(
            packed_in.at[by], packed_in.at[by], pack_send.at[by], pack_recv.at[by], peer(by)
        ).wait_recv()
    sums = [jnp.zeros((8, 640), F32)] * 8
    for by in range(REPS):
        values = jnp.dot(packed_in[by], spread_ref[...], preferred_element_type=F32)
        for k in range(4):
            numbers = kept_in[by, k : k + 1, :]
            for r in range(8):
                sums[r] += jnp.where(
                    numbers == column_block + 8 * r, values[8 * k : 8 * k + 8, :], 0.0
                )
    summed = jnp.concatenate(sums, axis=0)
    halfway = split_dot((table_ref[2, :64, :64], table_ref[3, :64, :64]), halves(summed))
    a, c = rep // 4, lax.rem(rep, 4)
    mine = weight_ref[
        pl.ds(pl.multiple_of(a * 64, 64), 64), pl.ds(pl.multiple_of(c * 640, 128), 640)
    ].astype(F32)
    for part in range(5):
        columns = slice(128 * part, 128 * part + 128)
        update = split_dot(
            halves(halfway[:, columns]), (table_ref[0, :128, :128], table_ref[1, :128, :128])
        )
        tile[:, columns] = (mine[:, columns] - (step_rate / REPS) * update).astype(BF16)

    def place(owner):
        return new_weight_ref.at[
            pl.ds(pl.multiple_of(owner // 4 * 64, 64), 64),
            pl.ds(pl.multiple_of(lax.rem(owner, 4) * 640, 128), 640),
        ]

    chip, core = rep // 2, lax.rem(rep, 2)
    twin = chip * 2 + 1 - core
    for by in range(0, 8):
        target = twin if by == 0 else lax.rem(chip + by, 8) * 2 + core
        copy = copy_to(tile, place(rep), tile_send.at[by], tile_recv.at[by], target)
        copy.start()
        sent.append(copy)
    own = place(rep)
    own[...] = tile[...]
    for by in range(1, 8):
        owner = lax.rem(chip + 8 - by, 8) * 2 + core
        copy_to(tile, place(owner), tile_send.at[by], tile_recv.at[by], twin).wait_recv()
        copy = copy_to(
            place(owner), place(owner), tile_send.at[by + 8], tile_recv.at[by + 8], twin
        )
        copy.start()
        sent.append(copy)
    copy_to(tile, place(twin), tile_send.at[0], tile_recv.at[0], twin).wait_recv()
    for by in range(1, 8):
        owner = lax.rem(chip + 8 - by, 8) * 2 + 1 - core
        copy_to(
            place(owner), place(owner), tile_send.at[by + 8], tile_recv.at[by + 8], twin
        ).wait_recv()
    for copy in sent:
        copy.wait_send()


def tables():
    n = np.arange(64, dtype=np.float64)
    scale = np.where(n == 0, np.sqrt(1.0 / 64.0), np.sqrt(2.0 / 64.0))
    cosine = scale[:, None] * np.cos(np.pi * (2.0 * n[None, :] + 1.0) * n[:, None] / 128.0)
    block = np.kron(np.eye(4), cosine).astype(np.float32)
    parts = []
    for matrix in (block, block.T):
        high = matrix.astype(BF16)
        parts += [high, (matrix - high.astype(np.float32)).astype(BF16)]
    column = np.arange(640)
    fold = np.zeros((640, 128), np.float32)
    fold[column, column // 64 * 8 + column % 8] = 1.0
    return np.stack(parts), fold.astype(BF16), np.ascontiguousarray(fold.T).astype(BF16)


def shards(tokens, out_grads, weight, momentum, kept_blocks):
    table, fold, spread = tables()
    gradient = reduced_gradient(out_grads, tokens)
    numbers = jnp.repeat(kept_blocks[0].transpose(0, 2, 1), 64, axis=2)
    numbers = jnp.pad(numbers, ((0, 0), (0, 4), (0, 0)))
    by_peer = numbers.reshape(4, 8, 4, 640).transpose(0, 2, 1, 3).reshape(16, 8, 640)
    return codec(gradient, momentum[0], numbers, by_peer, weight, table, fold, spread)


def codec(gradient, momentum, numbers, by_peer, weight, table, fold, spread):
    vmem = pl.BlockSpec(memory_space=pltpu.VMEM)
    dma = pltpu.SemaphoreType.DMA((REPS,))

    new_weight, new_momentum = pl.pallas_call(
        codec_kernel,
        out_shape=(
            jax.ShapeDtypeStruct((ROWS, D), BF16),
            jax.ShapeDtypeStruct((ROWS, D), BF16),
        ),
        in_specs=[vmem] * 8,
        out_specs=(vmem, vmem),
        scratch_shapes=[
            pltpu.VMEM((4, 32, D), BF16),
            pltpu.VMEM((REPS, 32, 128), BF16),
            pltpu.VMEM((REPS, 32, 128), BF16),
            pltpu.VMEM((REPS, 8, 640), jnp.int32),
            pltpu.VMEM((64, 640), BF16),
            dma, dma, dma, dma, dma, dma,
        ],
        compiler_params=pltpu.CompilerParams(
            collective_id=1, has_side_effects=True, vmem_limit_bytes=40 * 2**20
        ),
    )(gradient, momentum, numbers, by_peer, weight, table, fold, spread)
    return new_weight, new_momentum[None]


def solution(mesh):
    placed = (
        P(("rep", "fsdp"), None),
        P(("rep", "fsdp"), None),
        P("fsdp", None),
        P("rep", "fsdp", None),
        P("rep", "fsdp", None, None),
    )
    return jax.shard_map(
        shards,
        mesh=mesh,
        in_specs=placed,
        out_specs=(P("fsdp", None), P("rep", "fsdp", None)),
        check_vma=False,
    )
```

```python
import functools

import jax
import jax.numpy as jnp
import numpy as np
from jax import lax
from jax.experimental import pallas as pl
from jax.experimental.pallas import tpu as pltpu
from jax.sharding import PartitionSpec as P

beta_decay = 0.9
step_rate = 0.5

MESH = pl.DeviceIdType.MESH
F32 = jnp.float32
BF16 = jnp.bfloat16

D = 2560
ROWS = 256
SIDE = 4
REPS = 16

JOBS = (
    ("y", 0, 256),
    ("y", 512, 256),
    ("y", 1024, 256),
    ("y", 2048, 128),
    ("y", 2304, 128),
    ("z", 1536, 128),
    ("z", 1792, 128),
)
BATCHES = ((0, 512), (2048, 128))
ORDER = (
    ("far", 0), ("near", 0), ("near", 6), ("far", 1), ("far", 6), ("merge", 0), ("far", 5),
    ("merge", 6), ("near", 1), ("merge", 1), ("merge", 5), ("turn", 0), ("turn", 6), ("far", 2),
    ("relay", 0), ("near", 2), ("turn", 1), ("relay", 6), ("finish", 0), ("far", 3),
    ("relay", 1), ("merge", 2), ("near", 5), ("finish", 1), ("far", 4), ("finish", 6),
    ("near", 3), ("merge", 3), ("turn", 5), ("turn", 2), ("near", 4), ("merge", 4), ("relay", 2),
    ("turn", 3), ("relay", 5), ("finish", 2), ("relay", 3), ("finish", 3), ("turn", 4),
    ("finish", 5), ("pack", 0), ("relay", 4), ("decode", 0), ("finish", 4), ("pack", 1),
    ("spread", 0), ("decode", 1), ("spread", 1), ("gather", 0), ("gather", 1),
)


def split_dot(left, right):
    total = jnp.dot(left[0], right[0], preferred_element_type=F32)
    total += jnp.dot(left[0], right[1], preferred_element_type=F32)
    return total + jnp.dot(left[1], right[0], preferred_element_type=F32)


def halves(value):
    high = value.astype(BF16)
    return high, (value - high.astype(F32)).astype(BF16)


def iota(shape, axis):
    return lax.broadcasted_iota(jnp.int32, shape, axis)


def one_hot(where):
    return jnp.where(where, 1.0, 0.0).astype(BF16)


def step_kernel(
    g_hbm, t_hbm, mom_hbm, weight_hbm, table_hbm, own_ref, kept_ref,
    new_weight_ref, new_mom_ref,
    gt, stage, tokens, mom, grad, table, weight0, weight1,
    picked, packed, packed_in, kept_in, tile0, tile1, values, numbers_in,
    load_sem, send_sem, recv_sem, kept_send, kept_recv, pack_send, pack_recv,
    tile_send, tile_recv, *bufs,
):
    wide, thin = bufs[: len(JOBS)], bufs[len(JOBS) :]
    rep = lax.axis_index("rep")
    member = lax.axis_index("fsdp")
    pos = {"y": member // SIDE, "z": member % SIDE}
    chip, core = rep // 2, rep % 2
    place_x, place_z = chip // 2, chip % 2
    twin = chip * 2 + 1 - core

    def device(axis, index):
        if axis == "y":
            return (rep, index * SIDE + pos["z"])
        return (rep, pos["y"] * SIDE + index)

    def turn(index, by):
        return lax.rem(index + (by + SIDE), SIDE)

    def peer(by):
        return lax.rem(rep + by, REPS)

    row_tile, column_tile = rep // 4, rep % 4

    def tile_of(ref, batch, owner):
        first, width = BATCHES[batch]
        return ref.at[
            pl.ds(pl.multiple_of(owner // 4 * 64, 64), 64),
            pl.ds(pl.multiple_of(first + lax.rem(owner, 4) * width, 128), width),
        ]

    loads = {}

    def load(name, number, src, dst):
        loads[name] = pltpu.make_async_copy(src, dst, load_sem.at[number])
        loads[name].start()

    def load_group(block):
        group = turn(pos["y"], (2, 1, 3, 0)[block])
        columns = pl.ds(pl.multiple_of(group * 1024, 1024), 1024)
        load(block, block, g_hbm.at[:, columns], stage.at[block])

    load_group(0)
    load("t0", 4, t_hbm.at[:, :512], tokens.at[:, :512])
    for block in range(1, SIDE):
        load_group(block)
    load("t1", 5, t_hbm.at[:, 512:], tokens.at[:, 512:])
    load("mom", 6, mom_hbm, mom)
    load("table", 7, table_hbm, table)
    load("w0", 8, tile_of(weight_hbm, 0, rep), weight0)
    load("w1", 9, tile_of(weight_hbm, 1, rep), weight1)

    barrier = pltpu.get_barrier_semaphore()
    for axis in ("y", "z"):
        for by in (1, -1):
            pl.semaphore_signal(
                barrier, inc=1, device_id=device(axis, turn(pos[axis], by)), device_id_type=MESH
            )
    for by in range(1, REPS):
        pl.semaphore_signal(barrier, inc=1, device_id=(peer(by), member), device_id_type=MESH)

    def transpose(block):
        group = turn(pos["y"], (2, 1, 3, 0)[block])
        loads[block].wait()

        for part in range(SIDE):
            start = pl.multiple_of(group * 1024 + part * ROWS, ROWS)
            gt[pl.ds(start, ROWS), :] = stage[block, :, part * ROWS : part * ROWS + ROWS].T

    def partial(axis, group, other, column, width):
        owner = group * SIDE + other if axis == "y" else other * SIDE + group
        rows = pl.ds(pl.multiple_of(owner * ROWS, ROWS), ROWS)
        return jnp.dot(
            gt[rows, :], tokens[:, column : column + width], preferred_element_type=F32
        )

    sent = []

    def transfer(src, dst, sems, index, target):
        return pltpu.make_async_remote_copy(
            src_ref=src,
            dst_ref=dst,
            send_sem=sems[0].at[index],
            recv_sem=sems[1].at[index],
            device_id=target,
            device_id_type=MESH,
        )

    def send(*args):
        copy = transfer(*args)
        copy.start()
        sent.append(copy)

    def arrived(dst, sems, index):
        transfer(dst, dst, sems, index, (twin, member)).wait_recv()

    ring = (send_sem, recv_sem)
    kept_sems, pack_sems = (kept_send, kept_recv), (pack_send, pack_recv)
    tile_sems = (tile_send, tile_recv)

    def stage_outward(job, slot):
        axis, first, width = JOBS[job]
        m = pos[axis]
        for side, d in ((0, -1), (1, 1)):
            column = first + side * width
            buf = wide[job].at[side]
            group, target = (turn(m, 2), turn(m, d)) if slot == 0 else (turn(m, -d),) * 2
            for other in range(SIDE):
                buf[slot, other] = partial(axis, group, other, column, width).astype(BF16)
            send(buf.at[slot], buf.at[slot + 2], ring, (job, side, slot), device(axis, target))

    def stage_merge(job):
        axis, first, width = JOBS[job]
        m = pos[axis]
        for side, d in ((0, -1), (1, 1)):
            column = first + side * width
            buf = wide[job].at[side]
            arrived(buf.at[2], ring, (job, side, 0))

            for other in range(SIDE):
                total = partial(axis, turn(m, d), other, column, width)
                buf[2, other] = (total + buf[2, other].astype(F32)).astype(BF16)
            send(buf.at[2], buf.at[4], ring, (job, side, 2), device(axis, turn(m, d)))

    def stage_turn(job):
        axis, first, width = JOBS[job]
        other_axis = "z" if axis == "y" else "y"
        m, n = pos[axis], pos[other_axis]
        for side, d in ((0, -1), (1, 1)):
            column = first + side * width
            buf, low = wide[job].at[side], thin[job].at[side]
            arrived(buf.at[3], ring, (job, side, 1))
            arrived(buf.at[4], ring, (job, side, 2))
            for slot, other in ((0, turn(n, 2)), (1, turn(n, -d)), (2, turn(n, d)), (3, n)):
                total = (
                    partial(axis, m, other, column, width)
                    + buf[3, other].astype(F32)
                    + buf[4, other].astype(F32)
                )
                if slot == 3:
                    grad[:, column : column + width] = total
                else:
                    low[slot] = total.astype(BF16)
                if slot < 2:
                    target = turn(n, d) if slot == 0 else turn(n, -d)
                    send(
                        low.at[slot], low.at[slot + 3], ring, (job, side, slot + 3),
                        device(other_axis, target),
                    )

    def stage_relay(job):
        axis = "z" if JOBS[job][0] == "y" else "y"
        for side, d in ((0, -1), (1, 1)):
            low = thin[job].at[side]
            arrived(low.at[3], ring, (job, side, 3))
            low[3] = (low[2].astype(F32) + low[3].astype(F32)).astype(BF16)
            send(low.at[3], low.at[5], ring, (job, side, 5), device(axis, turn(pos[axis], d)))

    def stage_finish(job):
        _, first, width = JOBS[job]
        for side in (0, 1):
            arrived(thin[job].at[side, 4], ring, (job, side, 4))
            arrived(thin[job].at[side, 5], ring, (job, side, 5))
        forward = table[0, :width, :width], table[1, :width, :width]
        backward = table[2, :width, :width], table[3, :width, :width]
        position = (iota((1, width), 1) % 64) // 8

        @pl.loop(0, 2)
        def _(side):
            start = pl.multiple_of(first + side * width, 128)
            columns = pl.ds(start, width)
            low = thin[job].at[side]
            gradient = grad[:, columns] + low[4].astype(F32) + low[5].astype(F32)
            moment = beta_decay * mom[:, columns].astype(F32) + gradient
            halfway = split_dot((table[0], table[1]), halves(moment))
            coeffs = split_dot(halves(halfway), backward)
            span = start // 64 + iota((128, width), 1) // 64
            numbers = jnp.dot(
                own_ref[...].astype(F32).astype(BF16),
                one_hot(iota((128, width), 0) == span),
                preferred_element_type=F32,
            ).astype(jnp.int32)
            sparse_rows = []
            for a in range(4):
                folded = [jnp.zeros((8, width), F32)] * 4
                for r in range(8):
                    piece = coeffs[64 * a + 8 * r : 64 * a + 8 * r + 8, :]
                    kept = jnp.zeros((8, width), F32)
                    for k in range(4):
                        chosen = numbers[8 * a + k : 8 * a + k + 1, :] == position + 8 * r
                        one = jnp.where(chosen, piece, 0.0)
                        folded[k] += one
                        kept += one
                    sparse_rows.append(kept)
                picked[a, :, columns] = jnp.concatenate(folded, axis=0).astype(BF16)
            sparse = jnp.concatenate(sparse_rows, axis=0)
            halfway = split_dot((table[2], table[3]), halves(sparse))
            removed = split_dot(halves(halfway), forward)
            new_mom_ref[:, columns] = (moment - removed).astype(BF16)

    def stage_pack(batch):
        first, width = BATCHES[batch]
        column = iota((width, 128), 0)
        fold = one_hot(iota((width, 128), 1) == column // 64 * 8 + column % 8)
        for c in range(4):
            for a in range(4):
                packed[batch, a * 4 + c] = jnp.dot(
                    picked[a, :, first + width * c : first + width * c + width],
                    fold,
                    preferred_element_type=F32,
                ).astype(BF16)
        for by in range(1, REPS):
            send(
                packed.at[batch, peer(by)], packed_in.at[batch, by], pack_sems, (batch, by),
                (peer(by), member),
            )
        packed_in[batch, 0] = packed[batch, rep]

    def stage_decode(batch):
        width = BATCHES[batch][1]
        column = iota((128, width), 1)
        lane = iota((128, width), 0)
        if batch == 0:
            kept_in[0] = kept_ref[rep]
            for by in range(1, REPS):
                arrived(kept_in.at[by], kept_sems, (by,))
        for by in range(1, REPS):
            arrived(packed_in.at[batch, by], pack_sems, (batch, by))
        values[:, :width] = jnp.dot(
            packed_in[batch].reshape(REPS * 32, 128),
            one_hot(lane == column // 64 * 8 + column % 8),
            preferred_element_type=F32,
        )
        numbers_in[:, :width] = jnp.dot(
            kept_in[...].reshape(REPS * 8, 128).astype(F32).astype(BF16),
            one_hot(lane == 8 * batch + column // 64),
            preferred_element_type=F32,
        ).astype(jnp.int32)
        position = (iota((1, width), 1) % 64) // 8

        def add(r, sums):
            sums = list(sums)
            value = values[pl.ds(pl.multiple_of(r * 32, 32), 32), :width]
            number = numbers_in[pl.ds(pl.multiple_of(r * 8, 8), 8), :width]
            for k in range(4):
                for b in range(8):
                    sums[b] += jnp.where(
                        number[k : k + 1, :] == position + 8 * b, value[8 * k : 8 * k + 8, :], 0.0
                    )
            return tuple(sums)

        sums = lax.fori_loop(0, REPS, add, (jnp.zeros((8, width), F32),) * 8)
        summed = jnp.concatenate(sums, axis=0)
        halfway = split_dot((table[2, :64, :64], table[3, :64, :64]), halves(summed))
        weight, tile = ((weight0, tile0), (weight1, tile1))[batch]
        loads["w%d" % batch].wait()
        for part in range(width // 128):
            columns = slice(128 * part, 128 * part + 128)
            update = split_dot(
                halves(halfway[:, columns]), (table[0, :128, :128], table[1, :128, :128])
            )
            fresh = weight[:, columns].astype(F32) - (step_rate / REPS) * update
            tile[:, columns] = fresh.astype(BF16)
        own = tile_of(new_weight_ref, batch, rep)
        send(tile, own, tile_sems, (batch, 0), (twin, member))
        if batch == 0:
            send(tile, own, tile_sems, (batch, 1), (rep + 2 - 4 * place_z, member))
            for by in range(1, 4):
                send(tile, own, tile_sems, (batch, 1 + by), (lax.rem(rep + 4 * by, REPS), member))
        else:
            for by in range(1, 8):
                target = lax.rem(chip + by, 8) * 2 + core
                send(tile, own, tile_sems, (batch, by), (target, member))
        own[...] = tile[...]

    def sources(batch, of_core):
        if batch == 1:
            return [(by, lax.rem(chip + 8 - by, 8) * 2 + of_core) for by in range(1, 8)]
        found = [(1, place_x * 4 + (1 - place_z) * 2 + of_core)]
        for shift, level in ((1, place_z), (4, 1 - place_z)):
            for by in range(1, 4):
                owner = lax.rem(place_x + 4 - by, 4) * 4 + level * 2 + of_core
                found.append((shift + by, owner))
        return found

    def stage_spread(batch):
        for number, owner in sources(batch, core):
            part = tile_of(new_weight_ref, batch, owner)
            arrived(part, tile_sems, (batch, number))
            send(part, part, tile_sems, (batch, number + 7), (twin, member))
            if batch == 0 and number == 1:
                for by in range(1, 4):
                    target = lax.rem(rep + 4 * by, REPS)
                    send(part, part, tile_sems, (batch, 4 + by), (target, member))

    def stage_gather(batch):
        arrived(tile_of(new_weight_ref, batch, twin), tile_sems, (batch, 0))
        for number, owner in sources(batch, 1 - core):
            part = tile_of(new_weight_ref, batch, owner)
            arrived(part, tile_sems, (batch, number + 7))

    ready = set()

    def prepare(name, which):
        if name in ("far", "near", "merge", "turn"):
            axis = JOBS[which][0]
            blocks = {"far": (0,), "near": (1, 2), "merge": (1, 2), "turn": (3,)}[name]
            needs = list(blocks if axis == "y" else range(SIDE)) + ["t0"]
            needs += ["t1"] if JOBS[which][1] >= 512 else []
        else:
            needs = ["mom", "table"] if name == "finish" else []
        for need in needs:
            if need not in ready:
                ready.add(need)
                if need in range(SIDE):
                    transpose(need)
                else:
                    loads[need].wait()

    stages = {
        "far": lambda job: stage_outward(job, 0), "near": lambda job: stage_outward(job, 1),
        "merge": stage_merge, "turn": stage_turn, "relay": stage_relay, "finish": stage_finish,
        "pack": stage_pack, "decode": stage_decode, "spread": stage_spread,
        "gather": stage_gather,
    }
    prepare(*ORDER[0])
    pl.semaphore_wait(barrier, 4 + REPS - 1)
    for number, (name, which) in enumerate(ORDER):
        if number == 4:
            for by in range(1, REPS):
                send(kept_ref.at[peer(by)], kept_in.at[by], kept_sems, (by,), (peer(by), member))
        prepare(name, which)
        stages[name](which)
    for copy in sent:
        copy.wait_send()


def tables():
    n = np.arange(64, dtype=np.float64)
    scale = np.where(n == 0, np.sqrt(1.0 / 64.0), np.sqrt(2.0 / 64.0))
    cosine = scale[:, None] * np.cos(np.pi * (2.0 * n[None, :] + 1.0) * n[:, None] / 128.0)
    block = np.kron(np.eye(4), cosine).astype(np.float32)
    parts = []
    for matrix in (block, block.T):
        high = matrix.astype(BF16)
        parts += [high, (matrix - high.astype(np.float32)).astype(BF16)]
    return np.stack(parts)


def shards(tokens, out_grads, weight, momentum, kept_blocks):
    numbers = kept_blocks[0].transpose(0, 2, 1)
    own = jnp.pad(numbers, ((0, 0), (0, 4), (0, 88))).reshape(32, 128)
    peers = jnp.concatenate(
        [numbers[:, :, :32].reshape(4, 4, 4, 8), numbers[:, :, 32:].reshape(4, 4, 4, 2)], axis=3
    )
    peers = jnp.pad(peers.transpose(0, 2, 1, 3), ((0, 0), (0, 0), (0, 4), (0, 118)))
    vmem = pl.BlockSpec(memory_space=pltpu.VMEM)
    hbm = pl.BlockSpec(memory_space=pl.ANY)
    dma = pltpu.SemaphoreType.DMA
    new_weight, new_momentum = pl.pallas_call(
        step_kernel,
        out_shape=(
            jax.ShapeDtypeStruct((ROWS, D), BF16),
            jax.ShapeDtypeStruct((ROWS, D), BF16),
        ),
        in_specs=[hbm] * 5 + [vmem] * 2,
        out_specs=(vmem, vmem),
        scratch_shapes=[
            pltpu.VMEM((4096, 512), BF16),
            pltpu.VMEM((SIDE, 512, 1024), BF16),
            pltpu.VMEM((512, D), BF16),
            pltpu.VMEM((ROWS, D), BF16),
            pltpu.VMEM((ROWS, D), F32),
            pltpu.VMEM((4, 256, 256), BF16),
            pltpu.VMEM((64, 512), BF16),
            pltpu.VMEM((64, 128), BF16),
            pltpu.VMEM((4, 32, D), BF16),
            pltpu.VMEM((2, REPS, 32, 128), BF16),
            pltpu.VMEM((2, REPS, 32, 128), BF16),
            pltpu.VMEM((REPS, 8, 128), jnp.int32),
            pltpu.VMEM((64, 512), BF16),
            pltpu.VMEM((64, 128), BF16),
            pltpu.VMEM((REPS * 32, 512), F32),
            pltpu.VMEM((REPS * 8, 512), jnp.int32),
            dma((10,)),
            dma((len(JOBS), 2, 6)),
            dma((len(JOBS), 2, 6)),
            dma((REPS,)),
            dma((REPS,)),
            dma((2, REPS)),
            dma((2, REPS)),
            dma((2, REPS)),
            dma((2, REPS)),
        ]
        + [pltpu.VMEM((2, 5, SIDE, ROWS, job[2]), BF16) for job in JOBS]
        + [pltpu.VMEM((2, 6, ROWS, job[2]), BF16) for job in JOBS],
        compiler_params=pltpu.CompilerParams(
            collective_id=0, has_side_effects=True, vmem_limit_bytes=62 * 2**20
        ),
        cost_estimate=pl.CostEstimate(
            flops=2 * 512 * 4096 * D, bytes_accessed=2 * 512 * (4096 + D), transcendentals=0
        ),
    )(out_grads, tokens, momentum[0], weight, tables(), own, peers.reshape(REPS, 8, 128))
    return new_weight, new_momentum[None]


def solution(mesh):
    placed = (
        P(("rep", "fsdp"), None),
        P(("rep", "fsdp"), None),
        P("fsdp", None),
        P("rep", "fsdp", None),
        P("rep", "fsdp", None, None),
    )
    return jax.shard_map(
        shards,
        mesh=mesh,
        in_specs=placed,
        out_specs=(P("fsdp", None), P("rep", "fsdp", None)),
        check_vma=False,
    )
```

```python
import functools

import jax
import jax.numpy as jnp
import numpy as np
from jax import lax
from jax.experimental import pallas as pl
from jax.experimental.pallas import tpu as pltpu
from jax.sharding import PartitionSpec as P

beta_decay = 0.9
step_rate = 0.5

MESH = pl.DeviceIdType.MESH
F32 = jnp.float32
BF16 = jnp.bfloat16

D = 2560
ROWS = 256
SIDE = 4
REPS = 16

JOBS = (
    ("h", 0, 256),
    ("h", 256, 256),
    ("e", 512, 256),
    ("e", 768, 256),
    ("e", 1024, 256),
    ("e", 1280, 256),
    ("z", 1536, 256),
    ("e", 2048, 128),
    ("e", 2176, 128),
    ("e", 2304, 128),
    ("e", 2432, 128),
)
BATCHES = ((0, 512), (2048, 128))
ORDER = (
    ("tokens", 4), ("tokens", 3), ("inputs", 0), ("half", 0), ("far", 6), ("tokens", 9),
    ("half", 1), ("inputs", 1), ("near", 6), ("merge", 6), ("tokens", 2), ("quarter", 0),
    ("exchange", 4), ("exchange", 3), ("exchange", 9), ("tokens", 5), ("tokens", 7),
    ("quarter", 1), ("turn", 4), ("tokens", 8), ("tokens", 10), ("exchange", 2), ("turn", 6),
    ("turn", 3), ("relay", 4), ("turn", 9), ("turn", 0), ("relay", 3), ("relay", 9),
    ("exchange", 5), ("finish", 4), ("exchange", 7), ("turn", 2), ("relay", 0), ("finish", 3),
    ("finish", 9), ("turn", 1), ("relay", 2), ("exchange", 8), ("exchange", 10), ("turn", 5),
    ("finish", 0), ("relay", 6), ("relay", 1), ("turn", 7), ("relay", 5), ("turn", 8),
    ("finish", 2), ("finish", 1), ("turn", 10), ("relay", 7), ("finish", 6), ("finish", 5),
    ("relay", 8), ("pack", 0), ("relay", 10), ("decode", 0), ("finish", 8), ("finish", 7),
    ("finish", 10), ("pack", 1), ("spread", 0), ("decode", 1), ("spread", 1), ("gather", 0),
    ("gather", 1),
)


NEEDS = {
    "half": (0, 1), "quarter": (2,), "exchange": (0,), "turn": (3,), "far": (), "near": (),
    "merge": (),
}


def split_dot(left, right):
    total = jnp.dot(left[0], right[0], preferred_element_type=F32)
    total += jnp.dot(left[0], right[1], preferred_element_type=F32)
    return total + jnp.dot(left[1], right[0], preferred_element_type=F32)


def halves(value):
    high = value.astype(BF16)
    return high, (value - high.astype(F32)).astype(BF16)


def iota(shape, axis):
    return lax.broadcasted_iota(jnp.int32, shape, axis)


def one_hot(where):
    return jnp.where(where, 1.0, 0.0).astype(BF16)


def step_kernel(
    g_hbm, t_hbm, mom_hbm, weight_hbm, table_hbm, kept_ref,
    new_weight_ref, new_mom_ref,
    gt, gp, stage, tokens, tp, own_ref, mom, grad, table, weight0, weight1,
    picked, packed, packed_in, kept_in, tile0, tile1, values, numbers_in,
    load_sem, send_sem, recv_sem, pair_send, pair_recv, kept_send, kept_recv, pack_send, pack_recv,
    tile_send, tile_recv, *bufs,
):
    wide, thin = bufs[: len(JOBS)], bufs[len(JOBS) :]
    rep = lax.axis_index("rep")
    member = lax.axis_index("fsdp")
    pos = {"y": member // SIDE, "z": member % SIDE}
    chip, core = rep // 2, rep % 2
    place_x, place_z = chip // 2, chip % 2
    twin = chip * 2 + 1 - core

    def device(axis, index):
        if axis == "y":
            return (rep, index * SIDE + pos["z"])
        return (rep, pos["y"] * SIDE + index)

    def turn(index, by):
        return lax.rem(index + (by + SIDE), SIDE)

    def peer(by):
        return lax.rem(rep + by, REPS)

    row_tile, column_tile = rep // 4, rep % 4

    def tile_of(ref, batch, owner):
        first, width = BATCHES[batch]
        return ref.at[
            pl.ds(pl.multiple_of(owner // 4 * 64, 64), 64),
            pl.ds(pl.multiple_of(first + lax.rem(owner, 4) * width, 128), width),
        ]

    mate = pos["y"] + 1 - 2 * (pos["y"] % 2)
    other_mate = SIDE - 1 - pos["y"]
    groups = (other_mate, SIDE - 1 - mate, mate, pos["y"])

    loads = {}

    def load(name, number, src, dst):
        loads[name] = pltpu.make_async_copy(src, dst, load_sem.at[number])
        loads[name].start()

    def load_group(block):
        columns = pl.ds(pl.multiple_of(groups[block] * 1024, 1024), 1024)
        load(block, block, g_hbm.at[:, columns], stage.at[block])

    load_group(0)
    load("t0", 4, t_hbm.at[:, :512], tokens.at[:, :512])
    for block in range(1, SIDE):
        load_group(block)
    load("t1", 5, t_hbm.at[:, 512:], tokens.at[:, 512:])
    load("mom", 6, mom_hbm, mom)
    load("table", 7, table_hbm, table)
    load("w0", 8, tile_of(weight_hbm, 0, rep), weight0)
    load("w1", 9, tile_of(weight_hbm, 1, rep), weight1)

    barrier = pltpu.get_barrier_semaphore()
    for axis in ("y", "z"):
        for by in (1, -1):
            pl.semaphore_signal(
                barrier, inc=1, device_id=device(axis, turn(pos[axis], by)), device_id_type=MESH
            )
    for by in range(1, REPS):
        pl.semaphore_signal(barrier, inc=1, device_id=(peer(by), member), device_id_type=MESH)

    def transpose(block):
        group = groups[block]
        loads[block].wait()

        for part in range(SIDE):
            start = pl.multiple_of(group * 1024 + part * ROWS, ROWS)
            gt[pl.ds(start, ROWS), :] = stage[block, :, part * ROWS : part * ROWS + ROWS].T

    def partial(axis, group, other, column, width):
        owner = group * SIDE + other if axis == "y" else other * SIDE + group
        rows = pl.ds(pl.multiple_of(owner * ROWS, ROWS), ROWS)
        return jnp.dot(
            gt[rows, :], tokens[:, column : column + width], preferred_element_type=F32
        )

    def received(number, other, column, width):
        rows = pl.ds(pl.multiple_of(other * ROWS, ROWS), ROWS)
        return jnp.dot(
            gp[number, rows, :], tp[:, column : column + width], preferred_element_type=F32
        )

    def axes(job):
        return ("z", "y") if JOBS[job][0] == "z" else ("y", "z")

    def sides(job):
        kind, first, width = JOBS[job]
        if kind == "z":
            return ((0, first, -1), (1, first + width, 1))
        return ((0, first, -1 if job % 2 == 0 else 1),)

    sent = []

    def transfer(src, dst, sems, index, target):
        return pltpu.make_async_remote_copy(
            src_ref=src,
            dst_ref=dst,
            send_sem=sems[0].at[index],
            recv_sem=sems[1].at[index],
            device_id=target,
            device_id_type=MESH,
        )

    def send(*args):
        copy = transfer(*args)
        copy.start()
        sent.append(copy)

    def arrived(dst, sems, index):
        transfer(dst, dst, sems, index, (twin, member)).wait_recv()

    ring = (send_sem, recv_sem)
    pair_sems = (pair_send, pair_recv)
    kept_sems, pack_sems = (kept_send, kept_recv), (pack_send, pack_recv)
    tile_sems = (tile_send, tile_recv)

    def stage_inputs(number):
        start = pl.multiple_of(groups[1 + number] * 1024, 1024)
        send(
            gt.at[pl.ds(start, 1024), :], gp.at[number], pair_sems, (number,), device("y", mate)
        )

    def stage_tokens(job):
        _, first, width = JOBS[job]
        columns = slice(first, first + width)
        send(tokens.at[:, columns], tp.at[:, columns], pair_sems, (2 + job,), device("y", mate))

    def stage_half(job):
        _, first, width = JOBS[job]
        buf = wide[job]
        for slot in (0, 1):
            for other in range(SIDE):
                buf[slot, other] = partial("y", groups[slot], other, first, width).astype(BF16)
        send(buf.at[0:2], buf.at[2:4], ring, (job, 0, 0), device("y", other_mate))

    def stage_quarter(job):
        _, first, width = JOBS[job]
        buf = wide[job]
        arrived(buf.at[2:4], ring, (job, 0, 0))
        for other in range(SIDE):
            total = partial("y", mate, other, first, width)
            buf[3, other] = (total + buf[3, other].astype(F32)).astype(BF16)
        send(buf.at[3], buf.at[4], ring, (job, 0, 1), device("y", mate))

    def stage_exchange(job):
        _, first, width = JOBS[job]
        buf = wide[job]
        columns = slice(first, first + width)
        arrived(tp.at[:, columns], pair_sems, (2 + job,))
        for other in range(SIDE):
            total = partial("y", other_mate, other, first, width)
            buf[0, other] = (total + received(0, other, first, width)).astype(BF16)
        send(buf.at[0], buf.at[1], ring, (job, 0, 0), device("y", other_mate))

    def stage_outward(job, slot):
        width = JOBS[job][2]
        m = pos["z"]
        for side, column, d in sides(job):
            buf = wide[job].at[side]
            group, target = (turn(m, 2), turn(m, d)) if slot == 0 else (turn(m, -d),) * 2
            for other in range(SIDE):
                buf[slot, other] = partial("z", group, other, column, width).astype(BF16)
            send(buf.at[slot], buf.at[slot + 2], ring, (job, side, slot), device("z", target))

    def stage_merge(job):
        width = JOBS[job][2]
        m = pos["z"]
        for side, column, d in sides(job):
            buf = wide[job].at[side]
            arrived(buf.at[2], ring, (job, side, 0))
            for other in range(SIDE):
                total = partial("z", turn(m, d), other, column, width)
                buf[2, other] = (total + buf[2, other].astype(F32)).astype(BF16)
            send(buf.at[2], buf.at[4], ring, (job, side, 2), device("z", turn(m, d)))

    def stage_turn(job):
        kind, _, width = JOBS[job]
        axis, other_axis = axes(job)
        m, n = pos[axis], pos[other_axis]
        for side, column, d in sides(job):
            low = thin[job].at[side]
            if kind == "z":
                buf = wide[job].at[side]
                arrived(buf.at[3], ring, (job, side, 1))
                arrived(buf.at[4], ring, (job, side, 2))
                terms = (3, 4)
            elif kind == "h":
                buf = wide[job]
                arrived(buf.at[4], ring, (job, side, 1))
                terms = (2, 4)
            else:
                buf = wide[job]
                arrived(buf.at[1], ring, (job, side, 0))
                terms = (1,)
            for slot, other in ((0, turn(n, 2)), (1, turn(n, -d)), (2, turn(n, d)), (3, n)):
                total = partial(axis, m, other, column, width)
                if kind == "e":
                    total += received(1, other, column, width)
                for term in terms:
                    total += buf[term, other].astype(F32)
                if slot == 3:
                    grad[:, column : column + width] = total
                else:
                    low[slot] = total.astype(BF16)
                if slot < 2:
                    target = turn(n, d) if slot == 0 else turn(n, -d)
                    send(
                        low.at[slot], low.at[slot + 3], ring, (job, side, slot + 3),
                        device(other_axis, target),
                    )

    def stage_relay(job):
        axis = axes(job)[1]
        for side, column, d in sides(job):
            low = thin[job].at[side]
            arrived(low.at[3], ring, (job, side, 3))
            low[3] = (low[2].astype(F32) + low[3].astype(F32)).astype(BF16)
            send(low.at[3], low.at[5], ring, (job, side, 5), device(axis, turn(pos[axis], d)))

    def stage_finish(job):
        width = JOBS[job][2]
        backward = table[2, :width, :width], table[3, :width, :width]
        forward = table[0, :width, :width], table[1, :width, :width]
        position = (iota((1, width), 1) % 64) // 8
        for side, start, _ in sides(job):
            low = thin[job].at[side]
            arrived(low.at[4], ring, (job, side, 4))
            arrived(low.at[5], ring, (job, side, 5))
            columns = slice(start, start + width)
            gradient = grad[:, columns] + low[4].astype(F32) + low[5].astype(F32)
            moment = beta_decay * mom[:, columns].astype(F32) + gradient
            halfway = split_dot((table[0], table[1]), halves(moment))
            coeffs = split_dot(halves(halfway), backward)
            span = start // 64 + iota((128, width), 1) // 64
            numbers = jnp.dot(
                own_ref[...].astype(F32).astype(BF16),
                one_hot(iota((128, width), 0) == span),
                preferred_element_type=F32,
            ).astype(jnp.int32)
            sparse_rows = []
            for a in range(4):
                folded = [jnp.zeros((8, width), F32)] * 4
                for r in range(8):
                    piece = coeffs[64 * a + 8 * r : 64 * a + 8 * r + 8, :]
                    kept = jnp.zeros((8, width), F32)
                    for k in range(4):
                        chosen = numbers[8 * a + k : 8 * a + k + 1, :] == position + 8 * r
                        one = jnp.where(chosen, piece, 0.0)
                        folded[k] += one
                        kept += one
                    sparse_rows.append(kept)
                picked[a, :, columns] = jnp.concatenate(folded, axis=0).astype(BF16)
            sparse = jnp.concatenate(sparse_rows, axis=0)
            halfway = split_dot((table[2], table[3]), halves(sparse))
            removed = split_dot(halves(halfway), forward)
            new_mom_ref[:, columns] = (moment - removed).astype(BF16)

    def stage_pack(batch):
        first, width = BATCHES[batch]
        column = iota((width, 128), 0)
        fold = one_hot(iota((width, 128), 1) == column // 64 * 8 + column % 8)
        for c in range(4):
            for a in range(4):
                packed[batch, a * 4 + c] = jnp.dot(
                    picked[a, :, first + width * c : first + width * c + width],
                    fold,
                    preferred_element_type=F32,
                ).astype(BF16)
        for by in range(1, REPS):
            send(
                packed.at[batch, peer(by)], packed_in.at[batch, by], pack_sems, (batch, by),
                (peer(by), member),
            )
        packed_in[batch, 0] = packed[batch, rep]

    def stage_decode(batch):
        first, width = BATCHES[batch]
        column = iota((128, width), 1)
        lane = iota((128, width), 0)
        if batch == 0:
            kept_in[0] = own_ref[pl.ds(pl.multiple_of(row_tile * 8, 8), 8), :]
            for by in range(1, REPS):
                arrived(kept_in.at[by], kept_sems, (by,))
        for by in range(1, REPS):
            arrived(packed_in.at[batch, by], pack_sems, (batch, by))
        values[:, :width] = jnp.dot(
            packed_in[batch].reshape(REPS * 32, 128),
            one_hot(lane == column // 64 * 8 + column % 8),
            preferred_element_type=F32,
        )
        numbers_in[:, :width] = jnp.dot(
            kept_in[...].reshape(REPS * 8, 128).astype(F32).astype(BF16),
            one_hot(lane == (first + column_tile * width) // 64 + column // 64),
            preferred_element_type=F32,
        ).astype(jnp.int32)
        position = (iota((1, width), 1) % 64) // 8

        def add(r, sums):
            sums = list(sums)
            value = values[pl.ds(pl.multiple_of(r * 32, 32), 32), :width]
            number = numbers_in[pl.ds(pl.multiple_of(r * 8, 8), 8), :width]
            for k in range(4):
                for b in range(8):
                    sums[b] += jnp.where(
                        number[k : k + 1, :] == position + 8 * b, value[8 * k : 8 * k + 8, :], 0.0
                    )
            return tuple(sums)

        sums = lax.fori_loop(0, REPS, add, (jnp.zeros((8, width), F32),) * 8)
        summed = jnp.concatenate(sums, axis=0)
        halfway = split_dot((table[2, :64, :64], table[3, :64, :64]), halves(summed))
        weight, tile = ((weight0, tile0), (weight1, tile1))[batch]
        loads["w%d" % batch].wait()
        for part in range(width // 128):
            columns = slice(128 * part, 128 * part + 128)
            update = split_dot(
                halves(halfway[:, columns]), (table[0, :128, :128], table[1, :128, :128])
            )
            fresh = weight[:, columns].astype(F32) - (step_rate / REPS) * update
            tile[:, columns] = fresh.astype(BF16)
        own = tile_of(new_weight_ref, batch, rep)
        send(tile, own, tile_sems, (batch, 0), (twin, member))
        if batch == 0:
            send(tile, own, tile_sems, (batch, 1), (rep + 2 - 4 * place_z, member))
            for by in range(1, 4):
                send(tile, own, tile_sems, (batch, 1 + by), (lax.rem(rep + 4 * by, REPS), member))
        else:
            for by in range(1, 8):
                target = lax.rem(chip + by, 8) * 2 + core
                send(tile, own, tile_sems, (batch, by), (target, member))
        own[...] = tile[...]

    def sources(batch, of_core):
        if batch == 1:
            return [(by, lax.rem(chip + 8 - by, 8) * 2 + of_core) for by in range(1, 8)]
        found = [(1, place_x * 4 + (1 - place_z) * 2 + of_core)]
        for shift, level in ((1, place_z), (4, 1 - place_z)):
            for by in range(1, 4):
                owner = lax.rem(place_x + 4 - by, 4) * 4 + level * 2 + of_core
                found.append((shift + by, owner))
        return found

    def stage_spread(batch):
        for number, owner in sources(batch, core):
            part = tile_of(new_weight_ref, batch, owner)
            arrived(part, tile_sems, (batch, number))
            send(part, part, tile_sems, (batch, number + 7), (twin, member))
            if batch == 0 and number == 1:
                for by in range(1, 4):
                    target = lax.rem(rep + 4 * by, REPS)
                    send(part, part, tile_sems, (batch, 4 + by), (target, member))

    def stage_gather(batch):
        arrived(tile_of(new_weight_ref, batch, twin), tile_sems, (batch, 0))
        for number, owner in sources(batch, 1 - core):
            part = tile_of(new_weight_ref, batch, owner)
            arrived(part, tile_sems, (batch, number + 7))

    ready = set()

    def prepare(name, which):
        needs = []
        if name in NEEDS:
            needs = list(range(SIDE) if JOBS[which][0] == "z" else NEEDS[name])
            needs += ["t1" if JOBS[which][1] >= 512 else "t0"]
            if JOBS[which][0] == "e":
                needs += {"exchange": ["g0"], "turn": ["g1"]}[name]
        elif name == "inputs":
            needs = [1 + which]
        elif name == "tokens":
            needs = ["t1"]
        elif name == "finish":
            needs = ["mom", "table"]
        for need in needs:
            if need in ready:
                continue
            ready.add(need)
            if need in range(SIDE):
                transpose(need)
            elif need in ("g0", "g1"):
                number = int(need[1])
                arrived(gp.at[number], pair_sems, (number,))
            else:
                loads[need].wait()

    stages = {
        "inputs": stage_inputs, "tokens": stage_tokens, "half": stage_half,
        "quarter": stage_quarter, "exchange": stage_exchange,
        "far": lambda job: stage_outward(job, 0), "near": lambda job: stage_outward(job, 1),
        "merge": stage_merge, "turn": stage_turn, "relay": stage_relay, "finish": stage_finish,
        "pack": stage_pack, "decode": stage_decode, "spread": stage_spread,
        "gather": stage_gather,
    }
    own_ref[...] = jnp.zeros_like(own_ref)
    for a in range(4):
        own_ref[8 * a : 8 * a + 4, :40] = kept_ref[a]
    prepare("inputs", 0)
    pl.semaphore_wait(barrier, 4 + REPS - 1)
    for number, (name, which) in enumerate(ORDER):
        if number == 8:
            for by in range(1, REPS):
                rows = pl.ds(pl.multiple_of(peer(by) // 4 * 8, 8), 8)
                send(own_ref.at[rows, :], kept_in.at[by], kept_sems, (by,), (peer(by), member))
        prepare(name, which)
        stages[name](which)
    for copy in sent:
        copy.wait_send()


def tables():
    n = np.arange(64, dtype=np.float64)
    scale = np.where(n == 0, np.sqrt(1.0 / 64.0), np.sqrt(2.0 / 64.0))
    cosine = scale[:, None] * np.cos(np.pi * (2.0 * n[None, :] + 1.0) * n[:, None] / 128.0)
    block = np.kron(np.eye(4), cosine).astype(np.float32)
    parts = []
    for matrix in (block, block.T):
        high = matrix.astype(BF16)
        parts += [high, (matrix - high.astype(np.float32)).astype(BF16)]
    return np.stack(parts)


def shards(tokens, out_grads, weight, momentum, kept_blocks):
    numbers = kept_blocks[0].transpose(0, 2, 1)
    vmem = pl.BlockSpec(memory_space=pltpu.VMEM)
    hbm = pl.BlockSpec(memory_space=pl.ANY)
    dma = pltpu.SemaphoreType.DMA
    new_weight, new_momentum = pl.pallas_call(
        step_kernel,
        out_shape=(
            jax.ShapeDtypeStruct((ROWS, D), BF16),
            jax.ShapeDtypeStruct((ROWS, D), BF16),
        ),
        in_specs=[hbm] * 5 + [vmem],
        out_specs=(vmem, vmem),
        scratch_shapes=[
            pltpu.VMEM((4096, 512), BF16),
            pltpu.VMEM((2, 1024, 512), BF16),
            pltpu.VMEM((SIDE, 512, 1024), BF16),
            pltpu.VMEM((512, D), BF16),
            pltpu.VMEM((512, D), BF16),
            pltpu.VMEM((32, 128), jnp.int32),
            pltpu.VMEM((ROWS, D), BF16),
            pltpu.VMEM((ROWS, D), F32),
            pltpu.VMEM((4, 256, 256), BF16),
            pltpu.VMEM((64, 512), BF16),
            pltpu.VMEM((64, 128), BF16),
            pltpu.VMEM((4, 32, D), BF16),
            pltpu.VMEM((2, REPS, 32, 128), BF16),
            pltpu.VMEM((2, REPS, 32, 128), BF16),
            pltpu.VMEM((REPS, 8, 128), jnp.int32),
            pltpu.VMEM((64, 512), BF16),
            pltpu.VMEM((64, 128), BF16),
            pltpu.VMEM((REPS * 32, 512), F32),
            pltpu.VMEM((REPS * 8, 512), jnp.int32),
            dma((10,)),
            dma((len(JOBS), 2, 6)),
            dma((len(JOBS), 2, 6)),
            dma((2 + len(JOBS),)),
            dma((2 + len(JOBS),)),
            dma((REPS,)),
            dma((REPS,)),
            dma((2, REPS)),
            dma((2, REPS)),
            dma((2, REPS)),
            dma((2, REPS)),
        ]
        + [
            pltpu.VMEM({"h": (5,), "e": (2,), "z": (2, 5)}[kind] + (SIDE, ROWS, width), BF16)
            for kind, _, width in JOBS
        ]
        + [pltpu.VMEM((2 if kind == "z" else 1, 6, ROWS, width), BF16) for kind, _, width in JOBS],
        compiler_params=pltpu.CompilerParams(
            collective_id=0, has_side_effects=True, vmem_limit_bytes=52 * 2**20
        ),
        cost_estimate=pl.CostEstimate(
            flops=2 * 512 * 4096 * D, bytes_accessed=2 * 512 * (4096 + D), transcendentals=0
        ),
    )(out_grads, tokens, momentum[0], weight, tables(), numbers)
    return new_weight, new_momentum[None]


def solution(mesh):
    placed = (
        P(("rep", "fsdp"), None),
        P(("rep", "fsdp"), None),
        P("fsdp", None),
        P("rep", "fsdp", None),
        P("rep", "fsdp", None, None),
    )
    return jax.shard_map(
        shards,
        mesh=mesh,
        in_specs=placed,
        out_specs=(P("fsdp", None), P("rep", "fsdp", None)),
        check_vma=False,
    )
```

```python
import functools

import jax
import jax.numpy as jnp
import numpy as np
from jax import lax
from jax.experimental import pallas as pl
from jax.experimental.pallas import tpu as pltpu
from jax.sharding import PartitionSpec as P

beta_decay = 0.9
step_rate = 0.5

MESH = pl.DeviceIdType.MESH
F32 = jnp.float32
BF16 = jnp.bfloat16

D = 2560
ROWS = 256
SIDE = 4
REPS = 16

JOBS = (
    ("h", 0, 256),
    ("h", 256, 256),
    ("e", 512, 256),
    ("e", 768, 256),
    ("e", 1024, 256),
    ("e", 1280, 256),
    ("z", 1536, 256),
    ("e", 2048, 128),
    ("e", 2176, 128),
    ("e", 2304, 128),
    ("e", 2432, 128),
)
BATCHES = ((0, 512), (2048, 128))
ORDER = (
    ("tokens", 5), ("inputs", 0), ("half", 1), ("far", 6), ("near", 6), ("half", 0),
    ("tokens", 4), ("tokens", 3), ("inputs", 1), ("merge", 6), ("quarter", 1), ("exchange", 5),
    ("exchange", 4), ("exchange", 3), ("tokens", 2), ("quarter", 0), ("turn", 5), ("tokens", 9),
    ("tokens", 7), ("turn", 6), ("turn", 4), ("relay", 5), ("turn", 1), ("tokens", 10),
    ("tokens", 8), ("relay", 4), ("exchange", 2), ("turn", 3), ("finish", 5), ("finish", 4),
    ("turn", 0), ("relay", 1), ("exchange", 9), ("relay", 3), ("exchange", 7), ("turn", 2),
    ("relay", 6), ("relay", 0), ("turn", 9), ("exchange", 10), ("relay", 2), ("finish", 1),
    ("exchange", 8), ("turn", 7), ("finish", 6), ("finish", 3), ("finish", 0), ("turn", 10),
    ("finish", 2), ("pack", 0), ("relay", 7), ("relay", 9), ("turn", 8), ("relay", 10),
    ("relay", 8), ("finish", 7), ("decode", 0), ("finish", 9), ("finish", 10), ("finish", 8),
    ("pack", 1), ("spread", 0), ("decode", 1), ("spread", 1), ("gather", 0), ("gather", 1),
)


NEEDS = {
    "half": (0, 1), "quarter": (2,), "exchange": (0,), "turn": (3,), "far": (), "near": (),
    "merge": (),
}


def split_dot(left, right):
    total = jnp.dot(left[0], right[0], preferred_element_type=F32)
    total += jnp.dot(left[0], right[1], preferred_element_type=F32)
    return total + jnp.dot(left[1], right[0], preferred_element_type=F32)


def halves(value):
    high = value.astype(BF16)
    return high, (value - high.astype(F32)).astype(BF16)


def iota(shape, axis):
    return lax.broadcasted_iota(jnp.int32, shape, axis)


def one_hot(where):
    return jnp.where(where, 1.0, 0.0).astype(BF16)


def step_kernel(
    g_hbm, t_hbm, mom_hbm, weight_hbm, table_hbm, kept_ref,
    new_weight_ref, new_mom_ref,
    gt, gp, stage, tokens, tp, own_ref, mom, grad, table, weight0, weight1,
    picked, packed, packed_in, kept_in, tile0, tile1, values, numbers_in,
    load_sem, send_sem, recv_sem, pair_send, pair_recv, kept_send, kept_recv, pack_send, pack_recv,
    tile_send, tile_recv, *bufs,
):
    wide, thin = bufs[: len(JOBS)], bufs[len(JOBS) :]
    rep = lax.axis_index("rep")
    member = lax.axis_index("fsdp")
    pos = {"y": member // SIDE, "z": member % SIDE}
    chip, core = rep // 2, rep % 2
    place_x, place_z = chip // 2, chip % 2
    twin = chip * 2 + 1 - core

    def device(axis, index):
        if axis == "y":
            return (rep, index * SIDE + pos["z"])
        return (rep, pos["y"] * SIDE + index)

    def turn(index, by):
        return lax.rem(index + (by + SIDE), SIDE)

    def peer(by):
        return lax.rem(rep + by, REPS)

    row_tile, column_tile = rep // 4, rep % 4

    def tile_of(ref, batch, owner):
        first, width = BATCHES[batch]
        return ref.at[
            pl.ds(pl.multiple_of(owner // 4 * 64, 64), 64),
            pl.ds(pl.multiple_of(first + lax.rem(owner, 4) * width, 128), width),
        ]

    mate = pos["y"] + 1 - 2 * (pos["y"] % 2)
    other_mate = SIDE - 1 - pos["y"]
    groups = (other_mate, SIDE - 1 - mate, mate, pos["y"])

    loads = {}

    def load(name, number, src, dst):
        loads[name] = pltpu.make_async_copy(src, dst, load_sem.at[number])
        loads[name].start()

    def load_group(block):
        columns = pl.ds(pl.multiple_of(groups[block] * 1024, 1024), 1024)
        load(block, block, g_hbm.at[:, columns], stage.at[block])

    load_group(0)
    load("t0", 4, t_hbm.at[:, :512], tokens.at[:, :512])
    for block in range(1, SIDE):
        load_group(block)
    load("t1", 5, t_hbm.at[:, 512:], tokens.at[:, 512:])
    load("mom", 6, mom_hbm, mom)
    load("table", 7, table_hbm, table)
    load("w0", 8, tile_of(weight_hbm, 0, rep), weight0)
    load("w1", 9, tile_of(weight_hbm, 1, rep), weight1)

    barrier = pltpu.get_barrier_semaphore()
    for axis in ("y", "z"):
        for by in (1, -1):
            pl.semaphore_signal(
                barrier, inc=1, device_id=device(axis, turn(pos[axis], by)), device_id_type=MESH
            )
    for by in range(1, REPS):
        pl.semaphore_signal(barrier, inc=1, device_id=(peer(by), member), device_id_type=MESH)

    def transpose(block):
        group = groups[block]
        loads[block].wait()

        for part in range(SIDE):
            start = pl.multiple_of(group * 1024 + part * ROWS, ROWS)
            gt[pl.ds(start, ROWS), :] = stage[block, :, part * ROWS : part * ROWS + ROWS].T

    def partial(axis, group, other, column, width):
        owner = group * SIDE + other if axis == "y" else other * SIDE + group
        rows = pl.ds(pl.multiple_of(owner * ROWS, ROWS), ROWS)
        return jnp.dot(
            gt[rows, :], tokens[:, column : column + width], preferred_element_type=F32
        )

    def received(number, other, column, width):
        rows = pl.ds(pl.multiple_of(other * ROWS, ROWS), ROWS)
        return jnp.dot(
            gp[number, rows, :], tp[:, column : column + width], preferred_element_type=F32
        )

    def axes(job):
        return ("z", "y") if JOBS[job][0] == "z" else ("y", "z")

    def sides(job):
        kind, first, width = JOBS[job]
        if kind == "z":
            return ((0, first, -1), (1, first + width, 1))
        return ((0, first, -1 if job % 2 == 0 else 1),)

    sent = []

    def transfer(src, dst, sems, index, target):
        return pltpu.make_async_remote_copy(
            src_ref=src,
            dst_ref=dst,
            send_sem=sems[0].at[index],
            recv_sem=sems[1].at[index],
            device_id=target,
            device_id_type=MESH,
        )

    def send(*args):
        copy = transfer(*args)
        copy.start()
        sent.append(copy)

    def arrived(dst, sems, index):
        transfer(dst, dst, sems, index, (twin, member)).wait_recv()

    ring = (send_sem, recv_sem)
    pair_sems = (pair_send, pair_recv)
    kept_sems, pack_sems = (kept_send, kept_recv), (pack_send, pack_recv)
    tile_sems = (tile_send, tile_recv)

    def stage_inputs(number):
        start = pl.multiple_of(groups[1 + number] * 1024, 1024)
        send(
            gt.at[pl.ds(start, 1024), :], gp.at[number], pair_sems, (number,), device("y", mate)
        )

    def stage_tokens(job):
        _, first, width = JOBS[job]
        columns = slice(first, first + width)
        send(tokens.at[:, columns], tp.at[:, columns], pair_sems, (2 + job,), device("y", mate))

    def stage_half(job):
        _, first, width = JOBS[job]
        buf = wide[job]
        for slot in (0, 1):
            for other in range(SIDE):
                buf[slot, other] = partial("y", groups[slot], other, first, width).astype(BF16)
        send(buf.at[0:2], buf.at[2:4], ring, (job, 0, 0), device("y", other_mate))

    def stage_quarter(job):
        _, first, width = JOBS[job]
        buf = wide[job]
        arrived(buf.at[2:4], ring, (job, 0, 0))
        for other in range(SIDE):
            total = partial("y", mate, other, first, width)
            buf[3, other] = (total + buf[3, other].astype(F32)).astype(BF16)
        send(buf.at[3], buf.at[4], ring, (job, 0, 1), device("y", mate))

    def stage_exchange(job):
        _, first, width = JOBS[job]
        buf = wide[job]
        columns = slice(first, first + width)
        arrived(tp.at[:, columns], pair_sems, (2 + job,))
        for other in range(SIDE):
            total = partial("y", other_mate, other, first, width)
            buf[0, other] = (total + received(0, other, first, width)).astype(BF16)
        send(buf.at[0], buf.at[1], ring, (job, 0, 0), device("y", other_mate))

    def stage_outward(job, slot):
        width = JOBS[job][2]
        m = pos["z"]
        for side, column, d in sides(job):
            buf = wide[job].at[side]
            group, target = (turn(m, 2), turn(m, d)) if slot == 0 else (turn(m, -d),) * 2
            for other in range(SIDE):
                buf[slot, other] = partial("z", group, other, column, width).astype(BF16)
            send(buf.at[slot], buf.at[slot + 2], ring, (job, side, slot), device("z", target))

    def stage_merge(job):
        width = JOBS[job][2]
        m = pos["z"]
        for side, column, d in sides(job):
            buf = wide[job].at[side]
            arrived(buf.at[2], ring, (job, side, 0))
            for other in range(SIDE):
                total = partial("z", turn(m, d), other, column, width)
                buf[2, other] = (total + buf[2, other].astype(F32)).astype(BF16)
            send(buf.at[2], buf.at[4], ring, (job, side, 2), device("z", turn(m, d)))

    def stage_turn(job):
        kind, _, width = JOBS[job]
        axis, other_axis = axes(job)
        m, n = pos[axis], pos[other_axis]
        for side, column, d in sides(job):
            low = thin[job].at[side]
            if kind == "z":
                buf = wide[job].at[side]
                arrived(buf.at[3], ring, (job, side, 1))
                arrived(buf.at[4], ring, (job, side, 2))
                terms = (3, 4)
            elif kind == "h":
                buf = wide[job]
                arrived(buf.at[4], ring, (job, side, 1))
                terms = (2, 4)
            else:
                buf = wide[job]
                arrived(buf.at[1], ring, (job, side, 0))
                terms = (1,)
            for slot, other in ((0, turn(n, 2)), (1, turn(n, -d)), (2, turn(n, d)), (3, n)):
                total = partial(axis, m, other, column, width)
                if kind == "e":
                    total += received(1, other, column, width)
                for term in terms:
                    total += buf[term, other].astype(F32)
                if slot == 3:
                    grad[:, column : column + width] = total
                else:
                    low[slot] = total.astype(BF16)
                if slot < 2:
                    target = turn(n, d) if slot == 0 else turn(n, -d)
                    send(
                        low.at[slot], low.at[slot + 3], ring, (job, side, slot + 3),
                        device(other_axis, target),
                    )

    def stage_relay(job):
        axis = axes(job)[1]
        for side, column, d in sides(job):
            low = thin[job].at[side]
            arrived(low.at[3], ring, (job, side, 3))
            low[3] = (low[2].astype(F32) + low[3].astype(F32)).astype(BF16)
            send(low.at[3], low.at[5], ring, (job, side, 5), device(axis, turn(pos[axis], d)))

    def stage_finish(job):
        width = JOBS[job][2]
        backward = table[2, :width, :width], table[3, :width, :width]
        forward = table[0, :width, :width], table[1, :width, :width]
        position = (iota((1, width), 1) % 64) // 8
        for side, start, _ in sides(job):
            low = thin[job].at[side]
            arrived(low.at[4], ring, (job, side, 4))
            arrived(low.at[5], ring, (job, side, 5))
            columns = slice(start, start + width)
            gradient = grad[:, columns] + low[4].astype(F32) + low[5].astype(F32)
            moment = beta_decay * mom[:, columns].astype(F32) + gradient
            halfway = split_dot((table[0], table[1]), halves(moment))
            coeffs = split_dot(halves(halfway), backward)
            span = start // 64 + iota((128, width), 1) // 64
            numbers = jnp.dot(
                own_ref[...].astype(F32).astype(BF16),
                one_hot(iota((128, width), 0) == span),
                preferred_element_type=F32,
            ).astype(jnp.int32)
            sparse_rows = []
            for a in range(4):
                folded = [jnp.zeros((8, width), F32)] * 4
                for r in range(8):
                    piece = coeffs[64 * a + 8 * r : 64 * a + 8 * r + 8, :]
                    kept = jnp.zeros((8, width), F32)
                    for k in range(4):
                        chosen = numbers[8 * a + k : 8 * a + k + 1, :] == position + 8 * r
                        one = jnp.where(chosen, piece, 0.0)
                        folded[k] += one
                        kept += one
                    sparse_rows.append(kept)
                picked[a, :, columns] = jnp.concatenate(folded, axis=0).astype(BF16)
            sparse = jnp.concatenate(sparse_rows, axis=0)
            halfway = split_dot((table[2], table[3]), halves(sparse))
            removed = split_dot(halves(halfway), forward)
            new_mom_ref[:, columns] = (moment - removed).astype(BF16)

    def stage_pack(batch):
        first, width = BATCHES[batch]
        column = iota((width, 128), 0)
        fold = one_hot(iota((width, 128), 1) == column // 64 * 8 + column % 8)
        for c in range(4):
            for a in range(4):
                packed[batch, a * 4 + c] = jnp.dot(
                    picked[a, :, first + width * c : first + width * c + width],
                    fold,
                    preferred_element_type=F32,
                ).astype(BF16)
        for by in range(1, REPS):
            send(
                packed.at[batch, peer(by)], packed_in.at[batch, by], pack_sems, (batch, by),
                (peer(by), member),
            )
        packed_in[batch, 0] = packed[batch, rep]

    def stage_decode(batch):
        first, width = BATCHES[batch]
        column = iota((128, width), 1)
        lane = iota((128, width), 0)
        if batch == 0:
            kept_in[0] = own_ref[pl.ds(pl.multiple_of(row_tile * 8, 8), 8), :]
            for by in range(1, REPS):
                arrived(kept_in.at[by], kept_sems, (by,))
        for by in range(1, REPS):
            arrived(packed_in.at[batch, by], pack_sems, (batch, by))
        values[:, :width] = jnp.dot(
            packed_in[batch].reshape(REPS * 32, 128),
            one_hot(lane == column // 64 * 8 + column % 8),
            preferred_element_type=F32,
        )
        numbers_in[:, :width] = jnp.dot(
            kept_in[...].reshape(REPS * 8, 128).astype(F32).astype(BF16),
            one_hot(lane == (first + column_tile * width) // 64 + column // 64),
            preferred_element_type=F32,
        ).astype(jnp.int32)
        position = (iota((1, width), 1) % 64) // 8

        def add(r, sums):
            sums = list(sums)
            value = values[pl.ds(pl.multiple_of(r * 32, 32), 32), :width]
            number = numbers_in[pl.ds(pl.multiple_of(r * 8, 8), 8), :width]
            for k in range(4):
                for b in range(8):
                    sums[b] += jnp.where(
                        number[k : k + 1, :] == position + 8 * b, value[8 * k : 8 * k + 8, :], 0.0
                    )
            return tuple(sums)

        sums = lax.fori_loop(0, REPS, add, (jnp.zeros((8, width), F32),) * 8)
        summed = jnp.concatenate(sums, axis=0)
        halfway = split_dot((table[2, :64, :64], table[3, :64, :64]), halves(summed))
        weight, tile = ((weight0, tile0), (weight1, tile1))[batch]
        loads["w%d" % batch].wait()
        for part in range(width // 128):
            columns = slice(128 * part, 128 * part + 128)
            update = split_dot(
                halves(halfway[:, columns]), (table[0, :128, :128], table[1, :128, :128])
            )
            fresh = weight[:, columns].astype(F32) - (step_rate / REPS) * update
            tile[:, columns] = fresh.astype(BF16)
        own = tile_of(new_weight_ref, batch, rep)
        if batch == 0:
            send(tile, own, tile_sems, (batch, 0), (twin, member))
            send(tile, own, tile_sems, (batch, 1), (rep + 2 - 4 * place_z, member))
            for by in range(1, 4):
                send(tile, own, tile_sems, (batch, 1 + by), (lax.rem(rep + 4 * by, REPS), member))
        else:
            for by in range(1, REPS):
                send(tile, own, tile_sems, (batch, by), (peer(by), member))
        own[...] = tile[...]

    def sources(of_core):
        found = [(1, place_x * 4 + (1 - place_z) * 2 + of_core)]
        for shift, level in ((1, place_z), (4, 1 - place_z)):
            for by in range(1, 4):
                owner = lax.rem(place_x + 4 - by, 4) * 4 + level * 2 + of_core
                found.append((shift + by, owner))
        return found

    def stage_spread(batch):
        if batch == 1:
            for by in range(1, REPS):
                part = tile_of(new_weight_ref, batch, lax.rem(rep + REPS - by, REPS))
                arrived(part, tile_sems, (batch, by))
            return
        for number, owner in sources(core):
            part = tile_of(new_weight_ref, batch, owner)
            arrived(part, tile_sems, (batch, number))
            send(part, part, tile_sems, (batch, number + 7), (twin, member))
            if number == 1:
                for by in range(1, 4):
                    target = lax.rem(rep + 4 * by, REPS)
                    send(part, part, tile_sems, (batch, 4 + by), (target, member))

    def stage_gather(batch):
        if batch == 0:
            arrived(tile_of(new_weight_ref, batch, twin), tile_sems, (batch, 0))
            for number, owner in sources(1 - core):
                part = tile_of(new_weight_ref, batch, owner)
                arrived(part, tile_sems, (batch, number + 7))

    ready = set()

    def prepare(name, which):
        needs = []
        if name in NEEDS:
            needs = list(range(SIDE) if JOBS[which][0] == "z" else NEEDS[name])
            needs += ["t1" if JOBS[which][1] >= 512 else "t0"]
            if JOBS[which][0] == "e":
                needs += {"exchange": ["g0"], "turn": ["g1"]}[name]
        elif name == "inputs":
            needs = [1 + which]
        elif name == "tokens":
            needs = ["t1"]
        elif name == "finish":
            needs = ["mom", "table"]
        for need in needs:
            if need in ready:
                continue
            ready.add(need)
            if need in range(SIDE):
                transpose(need)
            elif need in ("g0", "g1"):
                number = int(need[1])
                arrived(gp.at[number], pair_sems, (number,))
            else:
                loads[need].wait()

    stages = {
        "inputs": stage_inputs, "tokens": stage_tokens, "half": stage_half,
        "quarter": stage_quarter, "exchange": stage_exchange,
        "far": lambda job: stage_outward(job, 0), "near": lambda job: stage_outward(job, 1),
        "merge": stage_merge, "turn": stage_turn, "relay": stage_relay, "finish": stage_finish,
        "pack": stage_pack, "decode": stage_decode, "spread": stage_spread,
        "gather": stage_gather,
    }
    own_ref[...] = jnp.zeros_like(own_ref)
    for a in range(4):
        own_ref[8 * a : 8 * a + 4, :40] = kept_ref[a]
    prepare("inputs", 0)
    pl.semaphore_wait(barrier, 4 + REPS - 1)
    for number, (name, which) in enumerate(ORDER):
        if number == 8:
            for by in range(1, REPS):
                rows = pl.ds(pl.multiple_of(peer(by) // 4 * 8, 8), 8)
                send(own_ref.at[rows, :], kept_in.at[by], kept_sems, (by,), (peer(by), member))
        prepare(name, which)
        stages[name](which)
    for copy in sent:
        copy.wait_send()


def tables():
    n = np.arange(64, dtype=np.float64)
    scale = np.where(n == 0, np.sqrt(1.0 / 64.0), np.sqrt(2.0 / 64.0))
    cosine = scale[:, None] * np.cos(np.pi * (2.0 * n[None, :] + 1.0) * n[:, None] / 128.0)
    block = np.kron(np.eye(4), cosine).astype(np.float32)
    parts = []
    for matrix in (block, block.T):
        high = matrix.astype(BF16)
        parts += [high, (matrix - high.astype(np.float32)).astype(BF16)]
    return np.stack(parts)


def shards(tokens, out_grads, weight, momentum, kept_blocks):
    numbers = kept_blocks[0].transpose(0, 2, 1)
    vmem = pl.BlockSpec(memory_space=pltpu.VMEM)
    hbm = pl.BlockSpec(memory_space=pltpu.HBM)
    dma = pltpu.SemaphoreType.DMA
    new_weight, new_momentum = pl.pallas_call(
        step_kernel,
        out_shape=(
            jax.ShapeDtypeStruct((ROWS, D), BF16),
            jax.ShapeDtypeStruct((ROWS, D), BF16),
        ),
        in_specs=[hbm] * 5 + [vmem],
        out_specs=(vmem, vmem),
        scratch_shapes=[
            pltpu.VMEM((4096, 512), BF16),
            pltpu.VMEM((2, 1024, 512), BF16),
            pltpu.VMEM((SIDE, 512, 1024), BF16),
            pltpu.VMEM((512, D), BF16),
            pltpu.VMEM((512, D), BF16),
            pltpu.VMEM((32, 128), jnp.int32),
            pltpu.VMEM((ROWS, D), BF16),
            pltpu.VMEM((ROWS, D), F32),
            pltpu.VMEM((4, 256, 256), BF16),
            pltpu.VMEM((64, 512), BF16),
            pltpu.VMEM((64, 128), BF16),
            pltpu.VMEM((4, 32, D), BF16),
            pltpu.VMEM((2, REPS, 32, 128), BF16),
            pltpu.VMEM((2, REPS, 32, 128), BF16),
            pltpu.VMEM((REPS, 8, 128), jnp.int32),
            pltpu.VMEM((64, 512), BF16),
            pltpu.VMEM((64, 128), BF16),
            pltpu.VMEM((REPS * 32, 512), F32),
            pltpu.VMEM((REPS * 8, 512), jnp.int32),
            dma((10,)),
            dma((len(JOBS), 2, 6)),
            dma((len(JOBS), 2, 6)),
            dma((2 + len(JOBS),)),
            dma((2 + len(JOBS),)),
            dma((REPS,)),
            dma((REPS,)),
            dma((2, REPS)),
            dma((2, REPS)),
            dma((2, REPS)),
            dma((2, REPS)),
        ]
        + [
            pltpu.VMEM({"h": (5,), "e": (2,), "z": (2, 5)}[kind] + (SIDE, ROWS, width), BF16)
            for kind, _, width in JOBS
        ]
        + [pltpu.VMEM((2 if kind == "z" else 1, 6, ROWS, width), BF16) for kind, _, width in JOBS],
        compiler_params=pltpu.CompilerParams(
            collective_id=0, has_side_effects=True, vmem_limit_bytes=52 * 2**20
        ),
        cost_estimate=pl.CostEstimate(
            flops=2 * 512 * 4096 * D, bytes_accessed=2 * 512 * (4096 + D), transcendentals=0
        ),
    )(out_grads, tokens, momentum[0], weight, tables(), numbers)
    return new_weight, new_momentum[None]


def solution(mesh):
    placed = (
        P(("rep", "fsdp"), None),
        P(("rep", "fsdp"), None),
        P("fsdp", None),
        P("rep", "fsdp", None),
        P("rep", "fsdp", None, None),
    )
    return jax.shard_map(
        shards,
        mesh=mesh,
        in_specs=placed,
        out_specs=(P("fsdp", None), P("rep", "fsdp", None)),
        check_vma=False,
    )
```

```python
import functools

import jax
import jax.numpy as jnp
import numpy as np
from jax import lax
from jax.experimental import pallas as pl
from jax.experimental.pallas import tpu as pltpu
from jax.sharding import PartitionSpec as P

beta_decay = 0.9
step_rate = 0.5

MESH = pl.DeviceIdType.MESH
F32 = jnp.float32
BF16 = jnp.bfloat16

D = 2560
ROWS = 256
SIDE = 4
REPS = 16

JOBS = (
    ("h", 0, 256),
    ("h", 256, 256),
    ("e", 512, 256),
    ("e", 768, 256),
    ("e", 1024, 256),
    ("e", 1280, 256),
    ("z", 1536, 256),
    ("e", 2048, 128),
    ("e", 2176, 128),
    ("e", 2304, 128),
    ("e", 2432, 128),
)
BATCHES = ((0, 512), (2048, 128))
ORDER = (
    ("far", 6), ("tokens", 4), ("tokens", 5), ("tokens", 2), ("near", 6), ("half", 0),
    ("inputs", 0), ("inputs", 1), ("half", 1), ("merge", 6), ("quarter", 0), ("exchange", 4),
    ("exchange", 5), ("exchange", 2), ("tokens", 3), ("quarter", 1), ("turn", 4), ("tokens", 9),
    ("tokens", 7), ("turn", 6), ("turn", 5), ("relay", 4), ("turn", 0), ("tokens", 8),
    ("tokens", 10), ("relay", 5), ("exchange", 3), ("turn", 2), ("finish", 4), ("relay", 0),
    ("finish", 5), ("turn", 1), ("exchange", 9), ("relay", 2), ("exchange", 7), ("turn", 3),
    ("relay", 6), ("relay", 1), ("finish", 0), ("turn", 9), ("exchange", 8), ("relay", 3),
    ("exchange", 10), ("turn", 7), ("finish", 6), ("relay", 9), ("finish", 2), ("finish", 1),
    ("turn", 8), ("finish", 3), ("pack", 0), ("relay", 7), ("turn", 10), ("relay", 8),
    ("finish", 9), ("relay", 10), ("decode", 0), ("finish", 7), ("finish", 8), ("finish", 10),
    ("pack", 1), ("pass", 0), ("decode", 1), ("spread", 0), ("spread", 1), ("gather", 0),
    ("gather", 1),
)


NEEDS = {
    "half": ((0, 1), ()), "quarter": ((2,), ()), "exchange": ((0,), ()), "turn": ((3,), (0,)),
    "far": ((), (2,)), "near": ((), (1, -1)), "merge": ((), (1, -1)),
}


def split_dot(left, right):
    total = jnp.dot(left[0], right[0], preferred_element_type=F32)
    total += jnp.dot(left[0], right[1], preferred_element_type=F32)
    return total + jnp.dot(left[1], right[0], preferred_element_type=F32)


def halves(value):
    high = value.astype(BF16)
    return high, (value - high.astype(F32)).astype(BF16)


def iota(shape, axis):
    return lax.broadcasted_iota(jnp.int32, shape, axis)


def one_hot(where):
    return jnp.where(where, 1.0, 0.0).astype(BF16)


def step_kernel(
    g_hbm, t_hbm, mom_hbm, weight_hbm, table_hbm, kept_ref,
    new_weight_ref, new_mom_ref,
    gt, gp, stage, tokens, tp, own_ref, mom, grad, table, weight0, weight1,
    picked, packed, packed_in, kept_in, tile0, tile1, values, numbers_in,
    load_sem, send_sem, recv_sem, pair_send, pair_recv, kept_send, kept_recv, pack_send, pack_recv,
    tile_send, tile_recv, *bufs,
):
    wide, thin = bufs[: len(JOBS)], bufs[len(JOBS) :]
    rep = lax.axis_index("rep")
    member = lax.axis_index("fsdp")
    pos = {"y": member // SIDE, "z": member % SIDE}
    chip, core = rep // 2, rep % 2
    place_x, place_z = chip // 2, chip % 2
    twin = chip * 2 + 1 - core

    def device(axis, index):
        if axis == "y":
            return (rep, index * SIDE + pos["z"])
        return (rep, pos["y"] * SIDE + index)

    def turn(index, by):
        return lax.rem(index + (by + SIDE), SIDE)

    def peer(by):
        return lax.rem(rep + by, REPS)

    row_tile, column_tile = rep // 4, rep % 4

    def tile_of(ref, batch, owner):
        first, width = BATCHES[batch]
        return ref.at[
            pl.ds(pl.multiple_of(owner // 4 * 64, 64), 64),
            pl.ds(pl.multiple_of(first + lax.rem(owner, 4) * width, 128), width),
        ]

    mate = pos["y"] + 1 - 2 * (pos["y"] % 2)
    other_mate = SIDE - 1 - pos["y"]
    groups = (other_mate, SIDE - 1 - mate, mate, pos["y"])

    loads = {}
    ready = set()

    def load(name, number, src, dst):
        loads[name] = pltpu.make_async_copy(src, dst, load_sem.at[number])
        loads[name].start()

    def load_group(block):
        columns = pl.ds(pl.multiple_of(groups[block] * 1024, 1024), 1024)
        load(block, block, g_hbm.at[:, columns], stage.at[block])

    load_group(0)
    load("t0", 4, t_hbm.at[:, :512], tokens.at[:, :512])
    for block in range(1, SIDE):
        load_group(block)
    load("t1", 5, t_hbm.at[:, 512:], tokens.at[:, 512:])
    load("mom", 6, mom_hbm, mom)
    load("table", 7, table_hbm, table)
    load("w0", 8, tile_of(weight_hbm, 0, rep), weight0)
    load("w1", 9, tile_of(weight_hbm, 1, rep), weight1)

    barrier = pltpu.get_barrier_semaphore()
    for axis in ("y", "z"):
        for by in (1, -1):
            pl.semaphore_signal(
                barrier, inc=1, device_id=device(axis, turn(pos[axis], by)), device_id_type=MESH
            )
    for by in range(1, REPS):
        pl.semaphore_signal(barrier, inc=1, device_id=(peer(by), member), device_id_type=MESH)

    def transpose(block, by):
        if block not in ready:
            ready.add(block)
            loads[block].wait()
        part = turn(pos["z"], by)
        rows = pl.ds(pl.multiple_of(groups[block] * 1024 + part * ROWS, ROWS), ROWS)
        columns = pl.ds(pl.multiple_of(part * ROWS, ROWS), ROWS)
        gt[rows, :] = stage[block, :, columns].T

    def partial(axis, group, other, column, width):
        owner = group * SIDE + other if axis == "y" else other * SIDE + group
        rows = pl.ds(pl.multiple_of(owner * ROWS, ROWS), ROWS)
        return jnp.dot(
            gt[rows, :], tokens[:, column : column + width], preferred_element_type=F32
        )

    def received(number, other, column, width):
        rows = pl.ds(pl.multiple_of(other * ROWS, ROWS), ROWS)
        return jnp.dot(
            gp[number, rows, :], tp[:, column : column + width], preferred_element_type=F32
        )

    def axes(job):
        return ("z", "y") if JOBS[job][0] == "z" else ("y", "z")

    def sides(job):
        kind, first, width = JOBS[job]
        if kind == "z":
            return ((0, first, -1), (1, first + width, 1))
        return ((0, first, -1 if job % 2 == 0 else 1),)

    sent = []

    def transfer(src, dst, sems, index, target):
        return pltpu.make_async_remote_copy(
            src_ref=src,
            dst_ref=dst,
            send_sem=sems[0].at[index],
            recv_sem=sems[1].at[index],
            device_id=target,
            device_id_type=MESH,
        )

    def send(*args):
        copy = transfer(*args)
        copy.start()
        sent.append(copy)

    def arrived(dst, sems, index):
        transfer(dst, dst, sems, index, (twin, member)).wait_recv()

    ring = (send_sem, recv_sem)
    pair_sems = (pair_send, pair_recv)
    kept_sems, pack_sems = (kept_send, kept_recv), (pack_send, pack_recv)
    tile_sems = (tile_send, tile_recv)

    def stage_inputs(number):
        start = pl.multiple_of(groups[1 + number] * 1024, 1024)
        send(
            gt.at[pl.ds(start, 1024), :], gp.at[number], pair_sems, (number,), device("y", mate)
        )

    def stage_tokens(job):
        _, first, width = JOBS[job]
        columns = slice(first, first + width)
        send(tokens.at[:, columns], tp.at[:, columns], pair_sems, (2 + job,), device("y", mate))

    def stage_half(job):
        _, first, width = JOBS[job]
        buf = wide[job]
        for slot in (0, 1):
            for other in range(SIDE):
                buf[slot, other] = partial("y", groups[slot], other, first, width).astype(BF16)
        send(buf.at[0:2], buf.at[2:4], ring, (job, 0, 0), device("y", other_mate))

    def stage_quarter(job):
        _, first, width = JOBS[job]
        buf = wide[job]
        arrived(buf.at[2:4], ring, (job, 0, 0))
        for other in range(SIDE):
            total = partial("y", mate, other, first, width)
            buf[3, other] = (total + buf[3, other].astype(F32)).astype(BF16)
        send(buf.at[3], buf.at[4], ring, (job, 0, 1), device("y", mate))

    def stage_exchange(job):
        _, first, width = JOBS[job]
        buf = wide[job]
        columns = slice(first, first + width)
        arrived(tp.at[:, columns], pair_sems, (2 + job,))
        for other in range(SIDE):
            total = partial("y", other_mate, other, first, width)
            buf[0, other] = (total + received(0, other, first, width)).astype(BF16)
        send(buf.at[0], buf.at[1], ring, (job, 0, 0), device("y", other_mate))

    def stage_outward(job, slot):
        width = JOBS[job][2]
        m = pos["z"]
        for side, column, d in sides(job):
            buf = wide[job].at[side]
            group, target = (turn(m, 2), turn(m, d)) if slot == 0 else (turn(m, -d),) * 2
            for other in range(SIDE):
                buf[slot, other] = partial("z", group, other, column, width).astype(BF16)
            send(buf.at[slot], buf.at[slot + 2], ring, (job, side, slot), device("z", target))

    def stage_merge(job):
        width = JOBS[job][2]
        m = pos["z"]
        for side, column, d in sides(job):
            buf = wide[job].at[side]
            arrived(buf.at[2], ring, (job, side, 0))
            for other in range(SIDE):
                total = partial("z", turn(m, d), other, column, width)
                buf[2, other] = (total + buf[2, other].astype(F32)).astype(BF16)
            send(buf.at[2], buf.at[4], ring, (job, side, 2), device("z", turn(m, d)))

    def stage_turn(job):
        kind, _, width = JOBS[job]
        axis, other_axis = axes(job)
        m, n = pos[axis], pos[other_axis]
        for side, column, d in sides(job):
            low = thin[job].at[side]
            if kind == "z":
                buf = wide[job].at[side]
                arrived(buf.at[3], ring, (job, side, 1))
                arrived(buf.at[4], ring, (job, side, 2))
                terms = (3, 4)
            elif kind == "h":
                buf = wide[job]
                arrived(buf.at[4], ring, (job, side, 1))
                terms = (2, 4)
            else:
                buf = wide[job]
                arrived(buf.at[1], ring, (job, side, 0))
                terms = (1,)
            for slot, other in ((0, turn(n, 2)), (1, turn(n, -d)), (2, turn(n, d)), (3, n)):
                total = partial(axis, m, other, column, width)
                if kind == "e":
                    total += received(1, other, column, width)
                for term in terms:
                    total += buf[term, other].astype(F32)
                if slot == 3:
                    grad[:, column : column + width] = total
                else:
                    low[slot] = total.astype(BF16)
                if slot < 2:
                    target = turn(n, d) if slot == 0 else turn(n, -d)
                    send(
                        low.at[slot], low.at[slot + 3], ring, (job, side, slot + 3),
                        device(other_axis, target),
                    )

    def stage_relay(job):
        axis = axes(job)[1]
        for side, column, d in sides(job):
            low = thin[job].at[side]
            arrived(low.at[3], ring, (job, side, 3))
            low[3] = (low[2].astype(F32) + low[3].astype(F32)).astype(BF16)
            send(low.at[3], low.at[5], ring, (job, side, 5), device(axis, turn(pos[axis], d)))

    def stage_finish(job):
        width = JOBS[job][2]
        backward = table[2, :width, :width], table[3, :width, :width]
        forward = table[0, :width, :width], table[1, :width, :width]
        position = (iota((1, width), 1) % 64) // 8
        for side, start, _ in sides(job):
            low = thin[job].at[side]
            arrived(low.at[4], ring, (job, side, 4))
            arrived(low.at[5], ring, (job, side, 5))
            columns = slice(start, start + width)
            gradient = grad[:, columns] + low[4].astype(F32) + low[5].astype(F32)
            moment = beta_decay * mom[:, columns].astype(F32) + gradient
            halfway = split_dot((table[0], table[1]), halves(moment))
            coeffs = split_dot(halves(halfway), backward)
            span = start // 64 + iota((128, width), 1) // 64
            numbers = jnp.dot(
                own_ref[...].astype(F32).astype(BF16),
                one_hot(iota((128, width), 0) == span),
                preferred_element_type=F32,
            ).astype(jnp.int32)
            sparse_rows = []
            for a in range(4):
                folded = [jnp.zeros((8, width), F32)] * 4
                for r in range(8):
                    piece = coeffs[64 * a + 8 * r : 64 * a + 8 * r + 8, :]
                    kept = jnp.zeros((8, width), F32)
                    for k in range(4):
                        chosen = numbers[8 * a + k : 8 * a + k + 1, :] == position + 8 * r
                        one = jnp.where(chosen, piece, 0.0)
                        folded[k] += one
                        kept += one
                    sparse_rows.append(kept)
                picked[a, :, columns] = jnp.concatenate(folded, axis=0).astype(BF16)
            sparse = jnp.concatenate(sparse_rows, axis=0)
            halfway = split_dot((table[2], table[3]), halves(sparse))
            removed = split_dot(halves(halfway), forward)
            new_mom_ref[:, columns] = (moment - removed).astype(BF16)

    def stage_pack(batch):
        first, width = BATCHES[batch]
        column = iota((width, 128), 0)
        fold = one_hot(iota((width, 128), 1) == column // 64 * 8 + column % 8)
        for c in range(4):
            for a in range(4):
                packed[batch, a * 4 + c] = jnp.dot(
                    picked[a, :, first + width * c : first + width * c + width],
                    fold,
                    preferred_element_type=F32,
                ).astype(BF16)
        for by in range(1, REPS):
            send(
                packed.at[batch, peer(by)], packed_in.at[batch, by], pack_sems, (batch, by),
                (peer(by), member),
            )
        packed_in[batch, 0] = packed[batch, rep]

    def stage_decode(batch):
        first, width = BATCHES[batch]
        column = iota((128, width), 1)
        lane = iota((128, width), 0)
        if batch == 0:
            kept_in[0] = own_ref[pl.ds(pl.multiple_of(row_tile * 8, 8), 8), :]
            for by in range(1, REPS):
                arrived(kept_in.at[by], kept_sems, (by,))
        for by in range(1, REPS):
            arrived(packed_in.at[batch, by], pack_sems, (batch, by))
        values[:, :width] = jnp.dot(
            packed_in[batch].reshape(REPS * 32, 128),
            one_hot(lane == column // 64 * 8 + column % 8),
            preferred_element_type=F32,
        )
        numbers_in[:, :width] = jnp.dot(
            kept_in[...].reshape(REPS * 8, 128).astype(F32).astype(BF16),
            one_hot(lane == (first + column_tile * width) // 64 + column // 64),
            preferred_element_type=F32,
        ).astype(jnp.int32)
        position = (iota((1, width), 1) % 64) // 8

        def add(r, sums):
            sums = list(sums)
            value = values[pl.ds(pl.multiple_of(r * 32, 32), 32), :width]
            number = numbers_in[pl.ds(pl.multiple_of(r * 8, 8), 8), :width]
            for k in range(4):
                for b in range(8):
                    sums[b] += jnp.where(
                        number[k : k + 1, :] == position + 8 * b, value[8 * k : 8 * k + 8, :], 0.0
                    )
            return tuple(sums)

        sums = lax.fori_loop(0, REPS, add, (jnp.zeros((8, width), F32),) * 8)
        summed = jnp.concatenate(sums, axis=0)
        halfway = split_dot((table[2, :64, :64], table[3, :64, :64]), halves(summed))
        weight, tile = ((weight0, tile0), (weight1, tile1))[batch]
        loads["w%d" % batch].wait()
        for part in range(width // 128):
            columns = slice(128 * part, 128 * part + 128)
            update = split_dot(
                halves(halfway[:, columns]), (table[0, :128, :128], table[1, :128, :128])
            )
            fresh = weight[:, columns].astype(F32) - (step_rate / REPS) * update
            tile[:, columns] = fresh.astype(BF16)
        own = tile_of(new_weight_ref, batch, rep)
        if batch == 0:
            send(tile, own, tile_sems, (batch, 0), (twin, member))
            send(tile, own, tile_sems, (batch, 1), (rep + 2 - 4 * place_z, member))
            for by in range(1, 4):
                send(tile, own, tile_sems, (batch, 1 + by), (lax.rem(rep + 4 * by, REPS), member))
        else:
            for by in range(1, REPS):
                send(tile, own, tile_sems, (batch, by), (peer(by), member))
        own[...] = tile[...]

    def sources(of_core):
        found = [(1, place_x * 4 + (1 - place_z) * 2 + of_core)]
        for shift, level in ((1, place_z), (4, 1 - place_z)):
            for by in range(1, 4):
                owner = lax.rem(place_x + 4 - by, 4) * 4 + level * 2 + of_core
                found.append((shift + by, owner))
        return found

    def stage_spread(batch):
        if batch == 1:
            for by in range(1, REPS):
                part = tile_of(new_weight_ref, batch, lax.rem(rep + REPS - by, REPS))
                arrived(part, tile_sems, (batch, by))
            return
        for number, owner in sources(core)[1:]:
            part = tile_of(new_weight_ref, batch, owner)
            arrived(part, tile_sems, (batch, number))
            send(part, part, tile_sems, (batch, number + 7), (twin, member))

    def stage_pass(batch):
        number, owner = sources(core)[0]
        part = tile_of(new_weight_ref, batch, owner)
        arrived(part, tile_sems, (batch, number))
        for by in range(1, 4):
            target = lax.rem(rep + 4 * by, REPS)
            send(part, part, tile_sems, (batch, 4 + by), (target, member))
        send(part, part, tile_sems, (batch, number + 7), (twin, member))

    def stage_gather(batch):
        if batch == 0:
            arrived(tile_of(new_weight_ref, batch, twin), tile_sems, (batch, 0))
            for number, owner in sources(1 - core):
                part = tile_of(new_weight_ref, batch, owner)
                arrived(part, tile_sems, (batch, number + 7))

    def prepare(name, which):
        needs = []
        every = (2, 1, -1, 0)
        if name in NEEDS:
            blocks, turns = NEEDS[name]
            if JOBS[which][0] == "z":
                blocks = range(SIDE)
            else:
                turns = every
            needs = [(block, by) for block in blocks for by in turns]
            needs += ["t1" if JOBS[which][1] >= 512 else "t0"]
            if JOBS[which][0] == "e":
                needs += {"exchange": ["g0"], "turn": ["g1"]}[name]
        elif name == "inputs":
            needs = [(1 + which, by) for by in every]
        elif name == "tokens":
            needs = ["t1"]
        elif name == "finish":
            needs = ["mom", "table"]
        for need in needs:
            if need in ready:
                continue
            ready.add(need)
            if isinstance(need, tuple):
                transpose(*need)
            elif need in ("g0", "g1"):
                number = int(need[1])
                arrived(gp.at[number], pair_sems, (number,))
            else:
                loads[need].wait()

    stages = {
        "inputs": stage_inputs, "tokens": stage_tokens, "half": stage_half,
        "quarter": stage_quarter, "exchange": stage_exchange,
        "far": lambda job: stage_outward(job, 0), "near": lambda job: stage_outward(job, 1),
        "merge": stage_merge, "turn": stage_turn, "relay": stage_relay, "finish": stage_finish,
        "pack": stage_pack, "decode": stage_decode, "spread": stage_spread, "pass": stage_pass,
        "gather": stage_gather,
    }
    own_ref[...] = jnp.zeros_like(own_ref)
    for a in range(4):
        own_ref[8 * a : 8 * a + 4, :40] = kept_ref[a]
    prepare("far", 6)
    pl.semaphore_wait(barrier, 4 + REPS - 1)
    for number, (name, which) in enumerate(ORDER):
        if number == 8:
            for by in range(1, REPS):
                rows = pl.ds(pl.multiple_of(peer(by) // 4 * 8, 8), 8)
                send(own_ref.at[rows, :], kept_in.at[by], kept_sems, (by,), (peer(by), member))
        prepare(name, which)
        stages[name](which)
    for copy in sent:
        copy.wait_send()


def tables():
    n = np.arange(64, dtype=np.float64)
    scale = np.where(n == 0, np.sqrt(1.0 / 64.0), np.sqrt(2.0 / 64.0))
    cosine = scale[:, None] * np.cos(np.pi * (2.0 * n[None, :] + 1.0) * n[:, None] / 128.0)
    block = np.kron(np.eye(4), cosine).astype(np.float32)
    parts = []
    for matrix in (block, block.T):
        high = matrix.astype(BF16)
        parts += [high, (matrix - high.astype(np.float32)).astype(BF16)]
    return np.stack(parts)


def shards(tokens, out_grads, weight, momentum, kept_blocks):
    numbers = kept_blocks[0].transpose(0, 2, 1)
    vmem = pl.BlockSpec(memory_space=pltpu.VMEM)
    hbm = pl.BlockSpec(memory_space=pltpu.HBM)
    dma = pltpu.SemaphoreType.DMA
    new_weight, new_momentum = pl.pallas_call(
        step_kernel,
        out_shape=(
            jax.ShapeDtypeStruct((ROWS, D), BF16),
            jax.ShapeDtypeStruct((ROWS, D), BF16),
        ),
        in_specs=[hbm] * 5 + [vmem],
        out_specs=(vmem, vmem),
        scratch_shapes=[
            pltpu.VMEM((4096, 512), BF16),
            pltpu.VMEM((2, 1024, 512), BF16),
            pltpu.VMEM((SIDE, 512, 1024), BF16),
            pltpu.VMEM((512, D), BF16),
            pltpu.VMEM((512, D), BF16),
            pltpu.VMEM((32, 128), jnp.int32),
            pltpu.VMEM((ROWS, D), BF16),
            pltpu.VMEM((ROWS, D), F32),
            pltpu.VMEM((4, 256, 256), BF16),
            pltpu.VMEM((64, 512), BF16),
            pltpu.VMEM((64, 128), BF16),
            pltpu.VMEM((4, 32, D), BF16),
            pltpu.VMEM((2, REPS, 32, 128), BF16),
            pltpu.VMEM((2, REPS, 32, 128), BF16),
            pltpu.VMEM((REPS, 8, 128), jnp.int32),
            pltpu.VMEM((64, 512), BF16),
            pltpu.VMEM((64, 128), BF16),
            pltpu.VMEM((REPS * 32, 512), F32),
            pltpu.VMEM((REPS * 8, 512), jnp.int32),
            dma((10,)),
            dma((len(JOBS), 2, 6)),
            dma((len(JOBS), 2, 6)),
            dma((2 + len(JOBS),)),
            dma((2 + len(JOBS),)),
            dma((REPS,)),
            dma((REPS,)),
            dma((2, REPS)),
            dma((2, REPS)),
            dma((2, REPS)),
            dma((2, REPS)),
        ]
        + [
            pltpu.VMEM({"h": (5,), "e": (2,), "z": (2, 5)}[kind] + (SIDE, ROWS, width), BF16)
            for kind, _, width in JOBS
        ]
        + [pltpu.VMEM((2 if kind == "z" else 1, 6, ROWS, width), BF16) for kind, _, width in JOBS],
        compiler_params=pltpu.CompilerParams(
            collective_id=0, has_side_effects=True, vmem_limit_bytes=52 * 2**20
        ),
        cost_estimate=pl.CostEstimate(
            flops=2 * 512 * 4096 * D, bytes_accessed=2 * 512 * (4096 + D), transcendentals=0
        ),
    )(out_grads, tokens, momentum[0], weight, tables(), numbers)
    return new_weight, new_momentum[None]


def solution(mesh):
    placed = (
        P(("rep", "fsdp"), None),
        P(("rep", "fsdp"), None),
        P("fsdp", None),
        P("rep", "fsdp", None),
        P("rep", "fsdp", None, None),
    )
    return jax.shard_map(
        shards,
        mesh=mesh,
        in_specs=placed,
        out_specs=(P("fsdp", None), P("rep", "fsdp", None)),
        check_vma=False,
    )
```

```python
import functools

import jax
import jax.numpy as jnp
import numpy as np
from jax import lax
from jax.experimental import pallas as pl
from jax.experimental.pallas import tpu as pltpu
from jax.sharding import PartitionSpec as P

beta_decay = 0.9
step_rate = 0.5

MESH = pl.DeviceIdType.MESH
F32 = jnp.float32
BF16 = jnp.bfloat16

D = 2560
ROWS = 256
SIDE = 4
REPS = 16

JOBS = (
    ("h", 0, 256),
    ("h", 256, 256),
    ("e", 512, 256),
    ("e", 768, 256),
    ("e", 1024, 256),
    ("e", 1280, 256),
    ("z", 1536, 256),
    ("e", 2048, 128),
    ("e", 2176, 128),
    ("e", 2304, 128),
    ("e", 2432, 128),
)
BATCHES = ((0, 512), (2048, 128))
ORDER = (
    ("far", 6), ("tokens", 4), ("tokens", 5), ("tokens", 2), ("near", 6), ("half", 0),
    ("inputs", 0), ("inputs", 1), ("half", 1), ("merge", 6), ("quarter", 0), ("exchange", 4),
    ("exchange", 5), ("exchange", 2), ("tokens", 3), ("quarter", 1), ("turn", 4), ("tokens", 9),
    ("tokens", 7), ("turn", 6), ("turn", 5), ("relay", 4), ("turn", 0), ("tokens", 8),
    ("tokens", 10), ("relay", 5), ("exchange", 3), ("turn", 2), ("finish", 4), ("relay", 0),
    ("finish", 5), ("turn", 1), ("exchange", 9), ("relay", 2), ("exchange", 7), ("turn", 3),
    ("relay", 6), ("relay", 1), ("finish", 0), ("turn", 9), ("exchange", 8), ("relay", 3),
    ("exchange", 10), ("turn", 7), ("finish", 6), ("relay", 9), ("finish", 2), ("finish", 1),
    ("turn", 8), ("finish", 3), ("pack", 0), ("relay", 7), ("turn", 10), ("relay", 8),
    ("finish", 9), ("relay", 10), ("decode", 0), ("finish", 7), ("finish", 8), ("finish", 10),
    ("pack", 1), ("pass", 0), ("decode", 1), ("spread", 0), ("spread", 1), ("gather", 0),
    ("gather", 1),
)


NEEDS = {
    "half": ((0, 1), ()), "quarter": ((2,), ()), "exchange": ((0,), ()), "turn": ((3,), (0,)),
    "far": ((), (2,)), "near": ((), (1, -1)), "merge": ((), (1, -1)),
}


def split_dot(left, right):
    total = jnp.dot(left[0], right[0], preferred_element_type=F32)
    total += jnp.dot(left[0], right[1], preferred_element_type=F32)
    return total + jnp.dot(left[1], right[0], preferred_element_type=F32)


def halves(value):
    high = value.astype(BF16)
    return high, (value - high.astype(F32)).astype(BF16)


def iota(shape, axis):
    return lax.broadcasted_iota(jnp.int32, shape, axis)


def one_hot(where):
    return jnp.where(where, 1.0, 0.0).astype(BF16)


def step_kernel(
    g_hbm, t_hbm, mom_hbm, weight_hbm, table_hbm, kept_hbm,
    new_weight_ref, new_mom_ref,
    gt, gp, stage, tokens, tp, kept_ref, own_ref, mom, grad, table, weight0, weight1,
    picked, packed, packed_in, kept_in, tile0, tile1, values, numbers_in,
    load_sem, send_sem, recv_sem, pair_send, pair_recv, kept_send, kept_recv, pack_send, pack_recv,
    tile_send, tile_recv, *bufs,
):
    wide, thin = bufs[: len(JOBS)], bufs[len(JOBS) :]
    rep = lax.axis_index("rep")
    member = lax.axis_index("fsdp")
    pos = {"y": member // SIDE, "z": member % SIDE}
    chip, core = rep // 2, rep % 2
    place_x, place_z = chip // 2, chip % 2
    twin = chip * 2 + 1 - core

    def device(axis, index):
        if axis == "y":
            return (rep, index * SIDE + pos["z"])
        return (rep, pos["y"] * SIDE + index)

    def turn(index, by):
        return lax.rem(index + (by + SIDE), SIDE)

    def peer(by):
        return lax.rem(rep + by, REPS)

    row_tile, column_tile = rep // 4, rep % 4

    def tile_of(ref, batch, owner):
        first, width = BATCHES[batch]
        return ref.at[
            pl.ds(pl.multiple_of(owner // 4 * 64, 64), 64),
            pl.ds(pl.multiple_of(first + lax.rem(owner, 4) * width, 128), width),
        ]

    mate = pos["y"] + 1 - 2 * (pos["y"] % 2)
    other_mate = SIDE - 1 - pos["y"]
    groups = (other_mate, SIDE - 1 - mate, mate, pos["y"])

    loads = {}
    ready = set()

    def load(name, number, src, dst):
        loads[name] = pltpu.make_async_copy(src, dst, load_sem.at[number])
        loads[name].start()

    def load_group(block):
        columns = pl.ds(pl.multiple_of(groups[block] * 1024, 1024), 1024)
        load(block, block, g_hbm.at[:, columns], stage.at[block])

    load_group(0)
    load("t0", 4, t_hbm.at[:, :512], tokens.at[:, :512])
    for block in range(1, SIDE):
        load_group(block)
    load("kept", 10, kept_hbm, kept_ref)
    load("t1", 5, t_hbm.at[:, 512:], tokens.at[:, 512:])
    load("mom", 6, mom_hbm, mom)
    load("table", 7, table_hbm, table)
    load("w0", 8, tile_of(weight_hbm, 0, rep), weight0)
    load("w1", 9, tile_of(weight_hbm, 1, rep), weight1)

    barrier = pltpu.get_barrier_semaphore()
    for axis in ("y", "z"):
        for by in (1, -1):
            pl.semaphore_signal(
                barrier, inc=1, device_id=device(axis, turn(pos[axis], by)), device_id_type=MESH
            )
    for by in range(1, REPS):
        pl.semaphore_signal(barrier, inc=1, device_id=(peer(by), member), device_id_type=MESH)

    def transpose(block, by):
        if block not in ready:
            ready.add(block)
            loads[block].wait()
        part = turn(pos["z"], by)
        rows = pl.ds(pl.multiple_of(groups[block] * 1024 + part * ROWS, ROWS), ROWS)
        columns = pl.ds(pl.multiple_of(part * ROWS, ROWS), ROWS)
        gt[rows, :] = stage[block, :, columns].T

    def partial(axis, group, other, column, width):
        owner = group * SIDE + other if axis == "y" else other * SIDE + group
        rows = pl.ds(pl.multiple_of(owner * ROWS, ROWS), ROWS)
        return jnp.dot(
            gt[rows, :], tokens[:, column : column + width], preferred_element_type=F32
        )

    def received(number, other, column, width):
        rows = pl.ds(pl.multiple_of(other * ROWS, ROWS), ROWS)
        return jnp.dot(
            gp[number, rows, :], tp[:, column : column + width], preferred_element_type=F32
        )

    def axes(job):
        return ("z", "y") if JOBS[job][0] == "z" else ("y", "z")

    def sides(job):
        kind, first, width = JOBS[job]
        if kind == "z":
            return ((0, first, -1), (1, first + width, 1))
        return ((0, first, -1 if job % 2 == 0 else 1),)

    sent = []

    def transfer(src, dst, sems, index, target):
        return pltpu.make_async_remote_copy(
            src_ref=src,
            dst_ref=dst,
            send_sem=sems[0].at[index],
            recv_sem=sems[1].at[index],
            device_id=target,
            device_id_type=MESH,
        )

    def send(*args):
        copy = transfer(*args)
        copy.start()
        sent.append(copy)

    def arrived(dst, sems, index):
        transfer(dst, dst, sems, index, (twin, member)).wait_recv()

    ring = (send_sem, recv_sem)
    pair_sems = (pair_send, pair_recv)
    kept_sems, pack_sems = (kept_send, kept_recv), (pack_send, pack_recv)
    tile_sems = (tile_send, tile_recv)

    def stage_inputs(number):
        start = pl.multiple_of(groups[1 + number] * 1024, 1024)
        send(
            gt.at[pl.ds(start, 1024), :], gp.at[number], pair_sems, (number,), device("y", mate)
        )

    def stage_tokens(job):
        _, first, width = JOBS[job]
        columns = slice(first, first + width)
        send(tokens.at[:, columns], tp.at[:, columns], pair_sems, (2 + job,), device("y", mate))

    def stage_half(job):
        _, first, width = JOBS[job]
        buf = wide[job]
        for slot in (0, 1):
            for other in range(SIDE):
                buf[slot, other] = partial("y", groups[slot], other, first, width).astype(BF16)
        send(buf.at[0:2], buf.at[2:4], ring, (job, 0, 0), device("y", other_mate))

    def stage_quarter(job):
        _, first, width = JOBS[job]
        buf = wide[job]
        arrived(buf.at[2:4], ring, (job, 0, 0))
        for other in range(SIDE):
            total = partial("y", mate, other, first, width)
            buf[3, other] = (total + buf[3, other].astype(F32)).astype(BF16)
        send(buf.at[3], buf.at[4], ring, (job, 0, 1), device("y", mate))

    def stage_exchange(job):
        _, first, width = JOBS[job]
        buf = wide[job]
        columns = slice(first, first + width)
        arrived(tp.at[:, columns], pair_sems, (2 + job,))
        for other in range(SIDE):
            total = partial("y", other_mate, other, first, width)
            buf[0, other] = (total + received(0, other, first, width)).astype(BF16)
        send(buf.at[0], buf.at[1], ring, (job, 0, 0), device("y", other_mate))

    def stage_outward(job, slot):
        width = JOBS[job][2]
        m = pos["z"]
        for side, column, d in sides(job):
            buf = wide[job].at[side]
            group, target = (turn(m, 2), turn(m, d)) if slot == 0 else (turn(m, -d),) * 2
            for other in range(SIDE):
                buf[slot, other] = partial("z", group, other, column, width).astype(BF16)
            send(buf.at[slot], buf.at[slot + 2], ring, (job, side, slot), device("z", target))

    def stage_merge(job):
        width = JOBS[job][2]
        m = pos["z"]
        for side, column, d in sides(job):
            buf = wide[job].at[side]
            arrived(buf.at[2], ring, (job, side, 0))
            for other in range(SIDE):
                total = partial("z", turn(m, d), other, column, width)
                buf[2, other] = (total + buf[2, other].astype(F32)).astype(BF16)
            send(buf.at[2], buf.at[4], ring, (job, side, 2), device("z", turn(m, d)))

    def stage_turn(job):
        kind, _, width = JOBS[job]
        axis, other_axis = axes(job)
        m, n = pos[axis], pos[other_axis]
        for side, column, d in sides(job):
            low = thin[job].at[side]
            if kind == "z":
                buf = wide[job].at[side]
                arrived(buf.at[3], ring, (job, side, 1))
                arrived(buf.at[4], ring, (job, side, 2))
                terms = (3, 4)
            elif kind == "h":
                buf = wide[job]
                arrived(buf.at[4], ring, (job, side, 1))
                terms = (2, 4)
            else:
                buf = wide[job]
                arrived(buf.at[1], ring, (job, side, 0))
                terms = (1,)
            for slot, other in ((0, turn(n, 2)), (1, turn(n, -d)), (2, turn(n, d)), (3, n)):
                total = partial(axis, m, other, column, width)
                if kind == "e":
                    total += received(1, other, column, width)
                for term in terms:
                    total += buf[term, other].astype(F32)
                if slot == 3:
                    grad[:, column : column + width] = total
                else:
                    low[slot] = total.astype(BF16)
                if slot < 2:
                    target = turn(n, d) if slot == 0 else turn(n, -d)
                    send(
                        low.at[slot], low.at[slot + 3], ring, (job, side, slot + 3),
                        device(other_axis, target),
                    )

    def stage_relay(job):
        axis = axes(job)[1]
        for side, column, d in sides(job):
            low = thin[job].at[side]
            arrived(low.at[3], ring, (job, side, 3))
            low[3] = (low[2].astype(F32) + low[3].astype(F32)).astype(BF16)
            send(low.at[3], low.at[5], ring, (job, side, 5), device(axis, turn(pos[axis], d)))

    def stage_finish(job):
        width = JOBS[job][2]
        backward = table[2, :width, :width], table[3, :width, :width]
        forward = table[0, :width, :width], table[1, :width, :width]
        position = (iota((1, width), 1) % 64) // 8
        for side, start, _ in sides(job):
            low = thin[job].at[side]
            arrived(low.at[4], ring, (job, side, 4))
            arrived(low.at[5], ring, (job, side, 5))
            columns = slice(start, start + width)
            gradient = grad[:, columns] + low[4].astype(F32) + low[5].astype(F32)
            moment = beta_decay * mom[:, columns].astype(F32) + gradient
            halfway = split_dot((table[0], table[1]), halves(moment))
            coeffs = split_dot(halves(halfway), backward)
            span = start // 64 + iota((128, width), 1) // 64
            numbers = jnp.dot(
                own_ref[...].astype(F32).astype(BF16),
                one_hot(iota((128, width), 0) == span),
                preferred_element_type=F32,
            ).astype(jnp.int32)
            sparse_rows = []
            for a in range(4):
                folded = [jnp.zeros((8, width), F32)] * 4
                for r in range(8):
                    piece = coeffs[64 * a + 8 * r : 64 * a + 8 * r + 8, :]
                    kept = jnp.zeros((8, width), F32)
                    for k in range(4):
                        chosen = numbers[8 * a + k : 8 * a + k + 1, :] == position + 8 * r
                        one = jnp.where(chosen, piece, 0.0)
                        folded[k] += one
                        kept += one
                    sparse_rows.append(kept)
                picked[a, :, columns] = jnp.concatenate(folded, axis=0).astype(BF16)
            sparse = jnp.concatenate(sparse_rows, axis=0)
            halfway = split_dot((table[2], table[3]), halves(sparse))
            removed = split_dot(halves(halfway), forward)
            new_mom_ref[:, columns] = (moment - removed).astype(BF16)

    def stage_pack(batch):
        first, width = BATCHES[batch]
        column = iota((width, 128), 0)
        fold = one_hot(iota((width, 128), 1) == column // 64 * 8 + column % 8)
        for c in range(4):
            for a in range(4):
                packed[batch, a * 4 + c] = jnp.dot(
                    picked[a, :, first + width * c : first + width * c + width],
                    fold,
                    preferred_element_type=F32,
                ).astype(BF16)
        for by in range(1, REPS):
            send(
                packed.at[batch, peer(by)], packed_in.at[batch, by], pack_sems, (batch, by),
                (peer(by), member),
            )
        packed_in[batch, 0] = packed[batch, rep]

    def stage_decode(batch):
        first, width = BATCHES[batch]
        column = iota((128, width), 1)
        lane = iota((128, width), 0)
        if batch == 0:
            kept_in[0] = own_ref[pl.ds(pl.multiple_of(row_tile * 8, 8), 8), :]
            for by in range(1, REPS):
                arrived(kept_in.at[by], kept_sems, (by,))
        for by in range(1, REPS):
            arrived(packed_in.at[batch, by], pack_sems, (batch, by))
        values[:, :width] = jnp.dot(
            packed_in[batch].reshape(REPS * 32, 128),
            one_hot(lane == column // 64 * 8 + column % 8),
            preferred_element_type=F32,
        )
        numbers_in[:, :width] = jnp.dot(
            kept_in[...].reshape(REPS * 8, 128).astype(F32).astype(BF16),
            one_hot(lane == (first + column_tile * width) // 64 + column // 64),
            preferred_element_type=F32,
        ).astype(jnp.int32)
        position = (iota((1, width), 1) % 64) // 8

        def add(r, sums):
            sums = list(sums)
            value = values[pl.ds(pl.multiple_of(r * 32, 32), 32), :width]
            number = numbers_in[pl.ds(pl.multiple_of(r * 8, 8), 8), :width]
            for k in range(4):
                for b in range(8):
                    sums[b] += jnp.where(
                        number[k : k + 1, :] == position + 8 * b, value[8 * k : 8 * k + 8, :], 0.0
                    )
            return tuple(sums)

        sums = lax.fori_loop(0, REPS, add, (jnp.zeros((8, width), F32),) * 8)
        summed = jnp.concatenate(sums, axis=0)
        halfway = split_dot((table[2, :64, :64], table[3, :64, :64]), halves(summed))
        weight, tile = ((weight0, tile0), (weight1, tile1))[batch]
        loads["w%d" % batch].wait()
        for part in range(width // 128):
            columns = slice(128 * part, 128 * part + 128)
            update = split_dot(
                halves(halfway[:, columns]), (table[0, :128, :128], table[1, :128, :128])
            )
            fresh = weight[:, columns].astype(F32) - (step_rate / REPS) * update
            tile[:, columns] = fresh.astype(BF16)
        own = tile_of(new_weight_ref, batch, rep)
        if batch == 0:
            send(tile, own, tile_sems, (batch, 0), (twin, member))
            send(tile, own, tile_sems, (batch, 1), (rep + 2 - 4 * place_z, member))
            for by in range(1, 4):
                send(tile, own, tile_sems, (batch, 1 + by), (lax.rem(rep + 4 * by, REPS), member))
        else:
            for by in range(1, REPS):
                send(tile, own, tile_sems, (batch, by), (peer(by), member))
        own[...] = tile[...]

    def sources(of_core):
        found = [(1, place_x * 4 + (1 - place_z) * 2 + of_core)]
        for shift, level in ((1, place_z), (4, 1 - place_z)):
            for by in range(1, 4):
                owner = lax.rem(place_x + 4 - by, 4) * 4 + level * 2 + of_core
                found.append((shift + by, owner))
        return found

    def stage_spread(batch):
        if batch == 1:
            for by in range(1, REPS):
                part = tile_of(new_weight_ref, batch, lax.rem(rep + REPS - by, REPS))
                arrived(part, tile_sems, (batch, by))
            return
        for number, owner in sources(core)[1:]:
            part = tile_of(new_weight_ref, batch, owner)
            arrived(part, tile_sems, (batch, number))
            send(part, part, tile_sems, (batch, number + 7), (twin, member))

    def stage_pass(batch):
        number, owner = sources(core)[0]
        part = tile_of(new_weight_ref, batch, owner)
        arrived(part, tile_sems, (batch, number))
        for by in range(1, 4):
            target = lax.rem(rep + 4 * by, REPS)
            send(part, part, tile_sems, (batch, 4 + by), (target, member))
        send(part, part, tile_sems, (batch, number + 7), (twin, member))

    def stage_gather(batch):
        if batch == 0:
            arrived(tile_of(new_weight_ref, batch, twin), tile_sems, (batch, 0))
            for number, owner in sources(1 - core):
                part = tile_of(new_weight_ref, batch, owner)
                arrived(part, tile_sems, (batch, number + 7))

    def prepare(name, which):
        needs = []
        every = (2, 1, -1, 0)
        if name in NEEDS:
            blocks, turns = NEEDS[name]
            if JOBS[which][0] == "z":
                blocks = range(SIDE)
            else:
                turns = every
            needs = [(block, by) for block in blocks for by in turns]
            needs += ["t1" if JOBS[which][1] >= 512 else "t0"]
            if JOBS[which][0] == "e":
                needs += {"exchange": ["g0"], "turn": ["g1"]}[name]
        elif name == "inputs":
            needs = [(1 + which, by) for by in every]
        elif name == "tokens":
            needs = ["t1"]
        elif name == "finish":
            needs = ["mom", "table"]
        for need in needs:
            if need in ready:
                continue
            ready.add(need)
            if isinstance(need, tuple):
                transpose(*need)
            elif need in ("g0", "g1"):
                number = int(need[1])
                arrived(gp.at[number], pair_sems, (number,))
            else:
                loads[need].wait()

    stages = {
        "inputs": stage_inputs, "tokens": stage_tokens, "half": stage_half,
        "quarter": stage_quarter, "exchange": stage_exchange,
        "far": lambda job: stage_outward(job, 0), "near": lambda job: stage_outward(job, 1),
        "merge": stage_merge, "turn": stage_turn, "relay": stage_relay, "finish": stage_finish,
        "pack": stage_pack, "decode": stage_decode, "spread": stage_spread, "pass": stage_pass,
        "gather": stage_gather,
    }
    own_ref[...] = jnp.zeros_like(own_ref)
    loads["kept"].wait()
    for a in range(4):
        own_ref[8 * a : 8 * a + 4, :40] = kept_ref[a]
    prepare("far", 6)
    pl.semaphore_wait(barrier, 4 + REPS - 1)
    for number, (name, which) in enumerate(ORDER):
        if number == 8:
            for by in range(1, REPS):
                rows = pl.ds(pl.multiple_of(peer(by) // 4 * 8, 8), 8)
                send(own_ref.at[rows, :], kept_in.at[by], kept_sems, (by,), (peer(by), member))
        prepare(name, which)
        stages[name](which)
    for copy in sent:
        copy.wait_send()


def tables():
    n = np.arange(64, dtype=np.float64)
    scale = np.where(n == 0, np.sqrt(1.0 / 64.0), np.sqrt(2.0 / 64.0))
    cosine = scale[:, None] * np.cos(np.pi * (2.0 * n[None, :] + 1.0) * n[:, None] / 128.0)
    block = np.kron(np.eye(4), cosine).astype(np.float32)
    parts = []
    for matrix in (block, block.T):
        high = matrix.astype(BF16)
        parts += [high, (matrix - high.astype(np.float32)).astype(BF16)]
    return np.stack(parts)


def shards(tokens, out_grads, weight, momentum, kept_blocks):
    numbers = kept_blocks[0].transpose(0, 2, 1)
    vmem = pl.BlockSpec(memory_space=pltpu.VMEM)
    hbm = pl.BlockSpec(memory_space=pltpu.HBM)
    dma = pltpu.SemaphoreType.DMA
    new_weight, new_momentum = pl.pallas_call(
        step_kernel,
        out_shape=(
            jax.ShapeDtypeStruct((ROWS, D), BF16),
            jax.ShapeDtypeStruct((ROWS, D), BF16),
        ),
        in_specs=[hbm] * 6,
        out_specs=(vmem, vmem),
        scratch_shapes=[
            pltpu.VMEM((4096, 512), BF16),
            pltpu.VMEM((2, 1024, 512), BF16),
            pltpu.VMEM((SIDE, 512, 1024), BF16),
            pltpu.VMEM((512, D), BF16),
            pltpu.VMEM((512, D), BF16),
            pltpu.VMEM((4, 4, 40), jnp.int32),
            pltpu.VMEM((32, 128), jnp.int32),
            pltpu.VMEM((ROWS, D), BF16),
            pltpu.VMEM((ROWS, D), F32),
            pltpu.VMEM((4, 256, 256), BF16),
            pltpu.VMEM((64, 512), BF16),
            pltpu.VMEM((64, 128), BF16),
            pltpu.VMEM((4, 32, D), BF16),
            pltpu.VMEM((2, REPS, 32, 128), BF16),
            pltpu.VMEM((2, REPS, 32, 128), BF16),
            pltpu.VMEM((REPS, 8, 128), jnp.int32),
            pltpu.VMEM((64, 512), BF16),
            pltpu.VMEM((64, 128), BF16),
            pltpu.VMEM((REPS * 32, 512), F32),
            pltpu.VMEM((REPS * 8, 512), jnp.int32),
            dma((11,)),
            dma((len(JOBS), 2, 6)),
            dma((len(JOBS), 2, 6)),
            dma((2 + len(JOBS),)),
            dma((2 + len(JOBS),)),
            dma((REPS,)),
            dma((REPS,)),
            dma((2, REPS)),
            dma((2, REPS)),
            dma((2, REPS)),
            dma((2, REPS)),
        ]
        + [
            pltpu.VMEM({"h": (5,), "e": (2,), "z": (2, 5)}[kind] + (SIDE, ROWS, width), BF16)
            for kind, _, width in JOBS
        ]
        + [pltpu.VMEM((2 if kind == "z" else 1, 6, ROWS, width), BF16) for kind, _, width in JOBS],
        compiler_params=pltpu.CompilerParams(
            collective_id=0, has_side_effects=True, vmem_limit_bytes=49 * 2**20
        ),
        cost_estimate=pl.CostEstimate(
            flops=2 * 512 * 4096 * D, bytes_accessed=2 * 512 * (4096 + D), transcendentals=0
        ),
    )(out_grads, tokens, momentum[0], weight, tables(), numbers)
    return new_weight, new_momentum[None]


def solution(mesh):
    placed = (
        P(("rep", "fsdp"), None),
        P(("rep", "fsdp"), None),
        P("fsdp", None),
        P("rep", "fsdp", None),
        P("rep", "fsdp", None, None),
    )
    return jax.shard_map(
        shards,
        mesh=mesh,
        in_specs=placed,
        out_specs=(P("fsdp", None), P("rep", "fsdp", None)),
        check_vma=False,
    )
```
